128 devices in a mesh: dp: 16 (over x_hi, y, core), vocab: 8 (over z, x_lo).
Axes of the slice: x: 4 (x_hi: 2, x_lo: 2; x = x_hi * 2 + x_lo), y: 4, z: 4, core: 2. Of those that a mesh axis runs over, the one named last changes fastest.
Arguments:
- teacher_hidden: bfloat16 [768, 4608], P('dp', 'vocab'), may hold values from -6 to 6
- teacher_gain: bfloat16 [4608], P('vocab'), may hold values from 0.25 to 1.75
- teacher_head: bfloat16 [131072, 4608], P(('dp', 'vocab')), as said below
- student_hidden: bfloat16 [768, 3584], P('dp', 'vocab'), may hold values from -0.59765625 to 0.59765625
- student_gain: bfloat16 [3584], P('vocab'), may hold values from 0.25 to 1.75
- student_table: bfloat16 [131072, 3584], P(('dp', 'vocab')), as said below
- embed_cot: bfloat16 [768, 3584], P('dp', 'vocab'), may hold values from -0.011962891 to 0.011962891
- token_ids: int32 [768], P('dp'), may hold values from 0 to 131071
Outputs:
- hidden_grad: bfloat16 [768, 3584], P('dp', 'vocab')
- table_grad: bfloat16 [131072, 3584], P(('dp', 'vocab'))
The draws below stay inside these ranges and needn't reach their ends.
Inputs may be any that keep to these rules, and one draw needn't show every extreme that they name: Each row of teacher_head and student_table is drawn independently. `student_table`: each row is drawn independently.
All inputs are finite; a program needn't handle non-finite values.
Results may differ from the reference program's by a relative error of at most 0.0087.
Values may be sent and summed in bfloat16 or wider, within the bound.
A program may use at most 192 MiB of HBM per device.

```python
import math
import jax
import jax.numpy as jnp
import numpy as np
from jax import lax

DT = 4608
DS = 3584
V = 131072
TOKENS = 768


def ramped(base, width):
    rows = base.shape[0]
    ramp = 1.0 + 0.09 * jnp.arange(rows, dtype=jnp.float32)[:, None] / rows
    return (base * ramp * (12.0 / width) ** 0.5).astype(jnp.bfloat16)


def draw_teacher_head(key, part):
    key = jax.random.fold_in(key, 11)
    base = jax.random.normal(key, (V, DT), jnp.float32)
    return ramped(base, DT)


def draw_student_table(key, part):
    key = jax.random.fold_in(key, 23)
    base = jax.random.normal(key, (V, DS), jnp.float32)
    return ramped(base, DS)


def set_ends(array, own_key, smallest, largest):
    place = [jax.random.randint(jax.random.fold_in(own_key, axis), (), 0, length) for axis, length in enumerate(array.shape)]
    longest = array.shape.index(max(array.shape))
    next_to = place[:longest] + [(place[longest] + 1) % array.shape[longest]] + place[longest + 1:]
    return array.at[tuple(place)].set(smallest).at[tuple(next_to)].set(largest)


def levels(key, shape, pieces, least, largest):
    level = 1.0
    for dim, shards_of in pieces:
        draws = jax.random.uniform(jax.random.fold_in(jax.random.fold_in(key, 6), dim), (shards_of,), jnp.float32, least / len(pieces), largest / len(pieces))
        level = level * jnp.repeat(jnp.exp(draws), shape[dim] // shards_of).reshape((-1,) + (1,) * (len(shape) - 1 - dim))
    return level


def wide_ids(own_key, shape, count, skew):
    weights = [min(1 << octave, count + 1 - (1 << octave)) * (1 << 20) // math.isqrt((1 << octave) ** skew) + 1 for octave in range((count + 1).bit_length()) if 1 << octave <= count]
    scale = 1 + sum(weights) // (1 << 30)
    table = np.cumsum(np.array([max(1, weight // scale) for weight in weights]))
    pick = jax.random.randint(jax.random.fold_in(own_key, 1), shape, 0, int(table[len(weights) - 1]))
    start = jnp.left_shift(1, jnp.searchsorted(jnp.asarray(table, jnp.int32), pick, side="right").astype(jnp.int32))
    standing = start - 1 + jax.random.randint(jax.random.fold_in(own_key, 4), shape, 0, 1 << 30) % jnp.minimum(start, count + 1 - start)
    return jax.random.permutation(jax.random.fold_in(own_key, 2), count)[standing].astype(jnp.int32)


def centred(stream_key, shape, deviation, bound, split=(), held_as=jnp.bfloat16):
    array = deviation * jax.random.normal(stream_key, shape, jnp.float32)
    if split:
        array = array * levels(stream_key, shape, split, -0.22, 0.18)
    return jnp.clip(array, -bound, bound).astype(held_as)


def setup_inputs(seed: int = 0) -> dict:
    streams_of = jax.random.split(jax.random.key(seed), 9)
    teacher_hidden = centred(streams_of[0], (TOKENS, DT), 1.0, 6.0, ((0, 16), (1, 8)))
    teacher_gain = jnp.clip(1.0 + 0.15 * jax.random.normal(streams_of[1], (DT,), jnp.float32), 0.25, 1.75).astype(jnp.bfloat16)
    teacher_head = draw_teacher_head(jax.random.fold_in(streams_of[8], 71), 0)
    student_hidden = centred(streams_of[3], (TOKENS, DS), 0.1, 0.59765625, ((0, 16), (1, 8)))
    student_gain = jnp.clip(1.0 + 0.15 * jax.random.normal(streams_of[4], (DS,), jnp.float32), 0.25, 1.75).astype(jnp.bfloat16)
    student_table = draw_student_table(jax.random.fold_in(streams_of[8], 71), 0)
    embed_cot = centred(streams_of[6], (TOKENS, DS), 0.002, 0.011962891, ((0, 16), (1, 8)))
    token_ids = set_ends(wide_ids(streams_of[7], (TOKENS,), V, 2), jax.random.fold_in(streams_of[7], 3), 0, V - 1).astype(jnp.int32)
    return dict(teacher_hidden=teacher_hidden, teacher_gain=teacher_gain, teacher_head=teacher_head, student_hidden=student_hidden, student_gain=student_gain, student_table=student_table, embed_cot=embed_cot, token_ids=token_ids)


def rms_norm(hidden, gain):
    values = hidden.astype(jnp.float32)
    scale = lax.rsqrt(lax.optimization_barrier(jnp.mean(values * values, axis=1, keepdims=True)) + 1e-06)
    return ((values * scale * gain.astype(jnp.float32)[None, :]).astype(jnp.bfloat16), scale)

def head_logits(normed, table):
    return lax.dot_general(normed, table, (((1,), (1,)), ((), ())), preferred_element_type=jnp.float32)

def reference(teacher_hidden, teacher_gain, teacher_head, student_hidden, student_gain, student_table, embed_cot, token_ids):
    t_normed, t_scale = rms_norm(teacher_hidden, teacher_gain)
    t_raw = head_logits(t_normed, teacher_head)
    t_exp = jnp.exp(30.0 * jnp.tanh(t_raw / 30.0))
    t_total = lax.optimization_barrier(jnp.sum(t_exp, axis=1, keepdims=True))
    s_normed, s_scale = rms_norm(student_hidden, student_gain)
    s_raw = head_logits(s_normed, student_table)
    s_tanh = jnp.tanh(s_raw / 30.0)
    s_exp = jnp.exp(30.0 * s_tanh)
    s_total = lax.optimization_barrier(jnp.sum(s_exp, axis=1, keepdims=True))
    logit_grad = ((s_exp / s_total - t_exp / t_total) * (1.0 - s_tanh * s_tanh)).astype(jnp.bfloat16)
    normed_grad = jnp.dot(logit_grad, student_table, preferred_element_type=jnp.float32)
    inner = lax.optimization_barrier(jnp.sum(normed_grad * s_normed.astype(jnp.float32), axis=1, keepdims=True))
    width = student_hidden.shape[1]
    hidden_grad = s_scale * student_gain.astype(jnp.float32)[None, :] * normed_grad
    hidden_grad = hidden_grad - student_hidden.astype(jnp.float32) * s_scale * s_scale * inner / width
    table_grad = lax.dot_general(logit_grad, s_normed, (((0,), (0,)), ((), ())), preferred_element_type=jnp.float32)
    table_grad = table_grad.at[token_ids].add(math.sqrt(width) * embed_cot.astype(jnp.float32))
    return (hidden_grad.astype(jnp.bfloat16), table_grad.astype(jnp.bfloat16))
```

```python
import math

import jax
import jax.numpy as jnp
from jax import lax
from jax.experimental import pallas as pl
from jax.experimental.pallas import tpu as pltpu
from jax.sharding import PartitionSpec as P

MESH = pl.DeviceIdType.MESH
F32, BF16 = jnp.float32, jnp.bfloat16
ORDER = (("z", "x", "y"), ("x", "y", "z"), ("y", "z", "x"))
NT = (((1,), (1,)), ((), ()))
NN = (((1,), (0,)), ((), ()))


def dot(a, b, dims=NN):
    return lax.dot_general(a, b, dims, preferred_element_type=F32)


class Place:
    def __init__(self):
        dp, vocab = lax.axis_index("dp"), lax.axis_index("vocab")
        self.vocab, self.dp = vocab, dp
        self.core = dp % 2
        self.at = {"x": (dp // 8) * 2 + vocab % 2, "y": (dp // 2) % 4, "z": vocab // 2}
        self.x_lo = vocab % 2

    def device(self, core=None, **moved):
        at = {**self.at, **moved}
        core = self.core if core is None else core
        return ((at["x"] // 2) * 8 + at["y"] * 2 + core, at["z"] * 2 + at["x"] % 2)

    def along(self, axis, by):
        return (self.at[axis] + by) % 4

    def shifted(self, axis, by):
        return self.device(**{axis: self.along(axis, by)})

    def sibling(self):
        return self.device(core=1 - self.core)


class Copies:
    def __init__(self, send_sems, recv_sems):
        self.send_sems, self.recv_sems, self.count, self.all = send_sems, recv_sems, 0, []

    def start(self, src, dst, device):
        copy = pltpu.make_async_remote_copy(
            src_ref=src,
            dst_ref=dst,
            send_sem=self.send_sems.at[self.count],
            recv_sem=self.recv_sems.at[self.count],
            device_id=device,
            device_id_type=MESH,
        )
        self.count += 1
        copy.start()
        self.all.append(copy)
        return copy


def region(fixed, core, part, lanes):
    whole = slice(None)
    z, y = fixed.get("z", whole), fixed.get("y", whole)
    x_lo, x_hi = (fixed["x"] % 2, fixed["x"] // 2) if "x" in fixed else (whole, whole)
    return (z, x_lo, x_hi, y, core, pl.ds(16 * part, 16), lanes)


def gather(here, copies, buf, width):
    low, high, full = pl.ds(0, width // 2), pl.ds(width // 2, width // 2), pl.ds(0, width)
    to_sibling = []

    def slab(p, ph, by, lanes, core=None):
        axis = ORDER[p][ph]
        fixed = {a: here.at[a] for a in "xyz" if a not in ORDER[p][:ph]}
        fixed[axis] = here.along(axis, by)
        return buf.at[region(fixed, here.core if core is None else core, p, lanes)]

    def push(p, ph, by, lanes, device):
        piece = slab(p, ph, by, lanes)
        return copies.start(piece, piece, device)

    for ph in range(3):
        first = []
        for p in range(3):
            axis = ORDER[p][ph]
            first.append(
                (push(p, ph, 0, full, here.shifted(axis, 1)), push(p, ph, 0, full, here.shifted(axis, -1)))
            )
        if ph == 2:
            to_sibling += [push(p, ph, 0, full, here.sibling()) for p in range(3)]
        yield
        second = []
        for p in range(3):
            axis = ORDER[p][ph]
            first[p][0].wait_recv()
            right = push(p, ph, -1, low, here.shifted(axis, 1))
            first[p][1].wait_recv()
            left = push(p, ph, 1, high, here.shifted(axis, -1))
            second.append((right, left))
        if ph == 2:
            to_sibling += [push(p, ph, by, full, here.sibling()) for p in range(3) for by in (-1, 1)]
        yield
        for p in range(3):
            for copy in second[p]:
                copy.wait_recv()
            if ph == 2:
                to_sibling.append(push(p, ph, 2, full, here.sibling()))
    yield
    for copy in to_sibling:
        copy.wait_recv()


def scatter(here, copies, buf, halves, wholes, result):
    low, high, full = pl.ds(0, 256), pl.ds(256, 256), pl.ds(0, 512)

    def slab(p, ph, by, lanes):
        order = ORDER[p][::-1]
        fixed = {a: here.at[a] for a in order[:ph]}
        fixed[order[ph]] = here.along(order[ph], by)
        return region(fixed, here.core, p, lanes)

    for ph in range(3):
        first = []
        for p in range(3):
            axis = ORDER[p][2 - ph]
            got = halves[p * 3 + ph]
            first.append(
                (
                    copies.start(buf.at[slab(p, ph, 2, low)], got.at[0], here.shifted(axis, 1)),
                    copies.start(buf.at[slab(p, ph, 2, high)], got.at[1], here.shifted(axis, -1)),
                )
            )
        yield
        second = []
        for p in range(3):
            axis = ORDER[p][2 - ph]
            got, into = halves[p * 3 + ph], wholes[p * 3 + ph]
            first[p][0].wait_recv()
            at = slab(p, ph, 1, low)
            buf[at] = (buf[at].astype(F32) + got[0].astype(F32)).astype(BF16)
            right = copies.start(buf.at[slab(p, ph, 1, full)], into.at[0], here.shifted(axis, 1))
            first[p][1].wait_recv()
            at = slab(p, ph, -1, high)
            buf[at] = (buf[at].astype(F32) + got[1].astype(F32)).astype(BF16)
            left = copies.start(buf.at[slab(p, ph, -1, full)], into.at[1], here.shifted(axis, -1))
            second.append((right, left))
        yield
        for p in range(3):
            into = wholes[p * 3 + ph]
            for copy in second[p]:
                copy.wait_recv()
            at = slab(p, ph, 0, full)
            total = buf[at].astype(F32) + into[0].astype(F32) + into[1].astype(F32)
            if ph < 2:
                buf[at] = total.astype(BF16)
            else:
                result[pl.ds(16 * p, 16), :] = total
    yield


def scatter_shapes():
    sizes = {"x": (2, 2), "y": (4,), "z": (4,)}
    halves, wholes = [], []
    for order in ORDER:
        left = ["x", "y", "z"]
        for axis in order[::-1]:
            left.remove(axis)
            dims = sum((sizes[a] for a in ("z", "x", "y") if a in left), ())
            halves.append(pltpu.VMEM((2, *dims, 16, 256), BF16))
            wholes.append(pltpu.VMEM((2, *dims, 16, 512), BF16))
    return halves, wholes


def column_to_row(column):
    rows, lanes = lax.broadcasted_iota(jnp.int32, (48, 128), 0), lax.broadcasted_iota(jnp.int32, (48, 128), 1)
    return jnp.sum(jnp.where(rows == lanes, column, 0.0), axis=0, keepdims=True)


def row_to_column(row):
    rows, lanes = lax.broadcasted_iota(jnp.int32, (48, 128), 0), lax.broadcasted_iota(jnp.int32, (48, 128), 1)
    return jnp.sum(jnp.where(rows == lanes, row, 0.0), axis=1, keepdims=True)


def vocab_start(here, copies, slots, first_row, second_row):
    rows = lax.broadcasted_iota(jnp.int32, (8, 128), 0)
    slots[here.vocab] = jnp.where(rows == 0, first_row, jnp.where(rows == 1, second_row, 0.0))
    mine = slots.at[here.vocab]
    return [copies.start(mine, mine, (here.dp, (here.vocab + by) % 8)) for by in range(1, 8)]


def vocab_sum(slots, started):
    for copy in started:
        copy.wait_recv()
    total = slots[0]
    for slot in range(1, 8):
        total = total + slots[slot]
    return total


def kernel(
    th_ref, tgain_ref, head_hbm, sh_ref, sgain_ref, table_hbm, ec_ref, ids_ref,
    hidden_grad_ref, table_grad_hbm,
    A, E, R, SB, HEAD, ST, EXPT, STANH, LGT, LG, OHT, GR, MSG, GOT, SQ, INNER, SCALE, TS, TR,
    *rest,
):
    halves, wholes, (send_sems, recv_sems, sib_send, sib_recv, load_sems, out_sems) = rest[:9], rest[9:18], rest[18:]
    here = Place()
    copies = Copies(send_sems, recv_sems)
    x_lo = here.x_lo
    width = 3584

    barrier = pltpu.get_barrier_semaphore()
    partners = [here.shifted(axis, by) for axis in "xyz" for by in (1, 2, 3)] + [here.sibling()]
    partners += [(here.dp, here.along("z", by) * 2 + 1 - x_lo) for by in (1, 2, 3)]
    for partner in partners:
        pl.semaphore_signal(barrier, inc=1, device_id=partner, device_id_type=MESH)

    load_head = pltpu.make_async_copy(head_hbm, HEAD, load_sems.at[0])
    load_table = pltpu.make_async_copy(table_hbm, ST, load_sems.at[1])
    load_head.start()
    load_table.start()

    th, sh, ec = th_ref[...].astype(F32), sh_ref[...].astype(F32), ec_ref[...].astype(F32)
    tgain, sgain = tgain_ref[...].astype(F32), sgain_ref[...].astype(F32)
    low = x_lo == 0
    MSG[0:48, :] = jnp.concatenate([jnp.where(low, sh, th[:, :448]), ec[:, :64]], axis=1).astype(BF16)
    gain_row = jnp.concatenate([jnp.where(low, sgain, tgain[:, :448]), jnp.zeros((1, 64), F32)], axis=1)
    MSG[48:64, :] = jnp.broadcast_to(gain_row, (16, 512)).astype(BF16)
    t_part = jnp.sum(th * th, axis=1, keepdims=True)
    s_part = jnp.sum(sh * sh, axis=1, keepdims=True)
    pl.semaphore_wait(barrier, len(partners))
    pair = copies.start(MSG, GOT, (here.dp, here.vocab + 1 - 2 * x_lo))
    started = vocab_start(here, copies, SQ, column_to_row(t_part), column_to_row(s_part))
    sums = vocab_sum(SQ, started)
    t_scale = lax.rsqrt(row_to_column(sums[0:1]) / 4608 + 1e-06)
    s_scale = lax.rsqrt(row_to_column(sums[1:2]) / width + 1e-06)
    SCALE[...] = jnp.broadcast_to(s_scale, (48, 128))
    pair.wait_recv()
    got = GOT[0:48, :].astype(F32)
    got_gain = GOT[48:64, :].astype(F32)[0:1]

    values = jnp.where(
        low,
        jnp.concatenate([th, got[:, :448]], axis=1),
        jnp.concatenate([th[:, 448:], got[:, :448], sh], axis=1),
    )
    gains = jnp.where(
        low,
        jnp.concatenate([tgain, got_gain[:, :448]], axis=1),
        jnp.concatenate([tgain[:, 448:], got_gain[:, :448], sgain], axis=1),
    )
    lanes = lax.broadcasted_iota(jnp.int32, (48, 1024), 1)
    scales = jnp.where(jnp.logical_or(low, lanes < 128), t_scale, s_scale)
    own = (here.at["z"], x_lo, here.at["x"] // 2, here.at["y"], here.core)
    A[own] = (values * scales * gains).astype(BF16)

    ids = ids_ref[...]
    spot = lax.broadcasted_iota(jnp.int32, (48, 128), 1)
    digits = jnp.where(
        spot == 0, ids // 4096, jnp.where(spot == 1, (ids // 64) % 64, jnp.where(spot == 2, ids % 64, 0))
    ).astype(F32)
    E[own] = jnp.where(
        low,
        jnp.concatenate([ec, got[:, 448:]], axis=1),
        jnp.concatenate([ec[:, 64:], digits], axis=1),
    ).astype(BF16)

    for _ in gather(here, copies, A, 1024):
        pass
    cotangents = gather(here, copies, E, 512)
    next(cotangents)

    def t_step(m, total):
        rows = pl.ds(pl.multiple_of(m * 256, 256), 256)
        raw = jnp.zeros((256, 768), F32)
        for z in range(4):
            at = z * 1152
            raw += dot(HEAD[rows, at : at + 1024], A[z, 0].reshape(768, 1024), NT)
            raw += dot(HEAD[rows, at + 1024 : at + 1152], A[z, 1, :, :, :, :, 0:128].reshape(768, 128), NT)
        value = jnp.exp(30.0 * jnp.tanh(raw * (1.0 / 30.0)))
        EXPT[rows, :] = value
        return total + jnp.sum(value, axis=0, keepdims=True)

    def s_step(m, total):
        rows = pl.ds(pl.multiple_of(m * 256, 256), 256)
        raw = jnp.zeros((256, 768), F32)
        for z in range(4):
            raw += dot(
                ST[rows, z * 896 : z * 896 + 896], A[z, 1, :, :, :, :, 128:1024].reshape(768, 896), NT
            )
        value = jnp.tanh(raw * (1.0 / 30.0))
        STANH[rows, :] = value
        return total + jnp.sum(jnp.exp(30.0 * value), axis=0, keepdims=True)

    load_head.wait()
    t_total = lax.fori_loop(0, 2, t_step, jnp.zeros((1, 768), F32))
    next(cotangents)
    t_total = lax.fori_loop(2, 4, t_step, t_total)
    next(cotangents)
    load_table.wait()
    s_total = lax.fori_loop(0, 2, s_step, jnp.zeros((1, 768), F32))
    next(cotangents)
    s_total = lax.fori_loop(2, 4, s_step, s_total)

    rows = lax.broadcasted_iota(jnp.int32, (8, 768), 0)
    TS[0] = jnp.where(rows == 0, t_total, s_total)
    slot = 0
    for step, axis in enumerate(("core", "x", "y", "z")):
        if axis == "core":
            targets = [here.sibling()]
        else:
            targets = [here.shifted(axis, by) for by in (1, 2, 3)]
        sent = [copies.start(TS.at[step], TR.at[slot + i], target) for i, target in enumerate(targets)]
        total = TS[step]
        for i, copy in enumerate(sent):
            copy.wait_recv()
            total = total + TR[slot + i]
        slot += len(targets)
        TS[step + 1] = total
    next(cotangents)
    inverse = 1.0 / TS[4]
    t_inverse, s_inverse = inverse[0:1], inverse[1:2]

    def grad_step(m, carry):
        rows = pl.ds(pl.multiple_of(m * 256, 256), 256)
        tanh = STANH[rows, :]
        grad = (jnp.exp(30.0 * tanh) * s_inverse - EXPT[rows, :] * t_inverse) * (1.0 - tanh * tanh)
        LGT[rows, :] = grad.astype(BF16)
        LG[:, rows] = grad.T.astype(BF16)
        return carry

    lax.fori_loop(0, 4, grad_step, 0)

    def to_sibling(z, x):
        return pltpu.make_async_remote_copy(
            src_ref=R.at[z, x, :, :, 1 - here.core],
            dst_ref=SB.at[z, x],
            send_sem=sib_send.at[z * 2 + x],
            recv_sem=sib_recv.at[z * 2 + x],
            device_id=here.sibling(),
            device_id_type=MESH,
        )

    def normed_grad_step(z, carry):
        for x in range(2):
            for half in range(2):
                columns = pl.ds(pl.multiple_of(z * 896 + x * 384 + half * 256, 128), 256)
                block = dot(LG[...], ST[:, columns]).astype(BF16)
                R[z, x, :, :, :, :, half * 256 : half * 256 + 256] = block.reshape(2, 4, 2, 48, 256)
            to_sibling(z, x).start()
        return carry

    lax.fori_loop(0, 2, normed_grad_step, 0)
    next(cotangents)
    lax.fori_loop(2, 4, normed_grad_step, 0)

    def sibling_sum_step(z, carry):
        for x in range(2):
            to_sibling(z, x).wait_recv()
            mine = R[z, x, :, :, here.core].astype(F32) + SB[z, x].astype(F32)
            R[z, x, :, :, here.core] = mine.astype(BF16)
        return carry

    lax.fori_loop(0, 4, sibling_sum_step, 0)
    next(cotangents)
    sums_over_chips = scatter(here, copies, R, halves, wholes, GR)
    next(sums_over_chips)
    for _ in cotangents:
        pass

    spot = lax.broadcasted_iota(jnp.int32, (8, 128), 1)
    weights = jnp.where(spot == 0, 4096.0, jnp.where(spot == 1, 64.0, jnp.where(spot == 2, 1.0, 0.0)))
    token_row = dot(weights.astype(BF16), E[0, 1, :, :, :, :, 384:512].reshape(768, 128), NT)[0:1]
    token_row = token_row - ((here.dp * 8 + here.vocab) * 1024).astype(F32)

    def one_hot_step(m, carry):
        rows = pl.ds(pl.multiple_of(m * 256, 256), 256)
        entry = (lax.broadcasted_iota(jnp.int32, (256, 768), 0) + m * 256).astype(F32)
        OHT[rows, :] = jnp.where(entry == token_row, 1.0, 0.0).astype(BF16)
        return carry

    lax.fori_loop(0, 4, one_hot_step, 0)

    def table_unit(z, x):
        size = 512 - 128 * x
        at = z * 896 + x * 512

        def step(m, carry):
            rows = pl.ds(pl.multiple_of(m * 512, 512), 512)
            states = A[z, 1, :, :, :, :, 128 + 512 * x : 128 + 512 * x + size].reshape(768, size)
            cots = E[z, x, :, :, :, :, 0:size].reshape(768, size)
            block = dot(LGT[rows, :], states) + math.sqrt(width) * dot(OHT[rows, :], cots)
            HEAD[rows, at : at + size] = block.astype(BF16)
            return carry

        lax.fori_loop(0, 2, step, 0)

    stores = []
    for z in range(4):
        table_unit(z, 0)
        next(sums_over_chips)
        table_unit(z, 1)
        columns = pl.ds(z * 896, 896)
        stores.append(
            pltpu.make_async_copy(HEAD.at[:, columns], table_grad_hbm.at[:, columns], out_sems.at[z])
        )
        stores[-1].start()
    for _ in sums_over_chips:
        pass

    found = GR[...]
    normed_grad = jnp.where(low, found[:, :448], found[:, 64:])
    s_scale = SCALE[:, 0:1]
    normed = (sh * s_scale * sgain).astype(BF16).astype(F32)
    row = column_to_row(jnp.sum(normed_grad * normed, axis=1, keepdims=True))
    inner = row_to_column(vocab_sum(INNER, vocab_start(here, copies, INNER, row, row))[0:1])
    hidden_grad = s_scale * sgain * normed_grad - sh * s_scale * s_scale * inner / width
    hidden_grad_ref[...] = hidden_grad.astype(BF16)

    for copy in copies.all:
        copy.wait_send()

    def sibling_sent_step(z, carry):
        for x in range(2):
            to_sibling(z, x).wait_send()
        return carry

    lax.fori_loop(0, 4, sibling_sent_step, 0)
    for store in stores:
        store.wait()


def per_device(th, tgain, head, sh, sgain, table, ec, ids):
    halves, wholes = scatter_shapes()
    vmem, hbm = pl.BlockSpec(memory_space=pltpu.VMEM), pl.BlockSpec(memory_space=pl.ANY)
    return pl.pallas_call(
        kernel,
        out_shape=(jax.ShapeDtypeStruct(sh.shape, BF16), jax.ShapeDtypeStruct(table.shape, BF16)),
        in_specs=[vmem, vmem, hbm, vmem, vmem, hbm, vmem, vmem],
        out_specs=(vmem, hbm),
        scratch_shapes=[
            pltpu.VMEM((4, 2, 2, 4, 2, 48, 1024), BF16),
            pltpu.VMEM((4, 2, 2, 4, 2, 48, 512), BF16),
            pltpu.VMEM((4, 2, 2, 4, 2, 48, 512), BF16),
            pltpu.VMEM((4, 2, 2, 4, 48, 512), BF16),
            pltpu.VMEM(head.shape, BF16),
            pltpu.VMEM(table.shape, BF16),
            pltpu.VMEM((1024, 768), F32),
            pltpu.VMEM((1024, 768), F32),
            pltpu.VMEM((1024, 768), BF16),
            pltpu.VMEM((768, 1024), BF16),
            pltpu.VMEM((1024, 768), BF16),
            pltpu.VMEM((48, 512), F32),
            pltpu.VMEM((64, 512), BF16),
            pltpu.VMEM((64, 512), BF16),
            pltpu.VMEM((8, 8, 128), F32),
            pltpu.VMEM((8, 8, 128), F32),
            pltpu.VMEM((48, 128), F32),
            pltpu.VMEM((5, 8, 768), F32),
            pltpu.VMEM((10, 8, 768), F32),
            *halves,
            *wholes,
            pltpu.SemaphoreType.DMA((192,)),
            pltpu.SemaphoreType.DMA((192,)),
            pltpu.SemaphoreType.DMA((8,)),
            pltpu.SemaphoreType.DMA((8,)),
            pltpu.SemaphoreType.DMA((2,)),
            pltpu.SemaphoreType.DMA((4,)),
        ],
        compiler_params=pltpu.CompilerParams(
            collective_id=0, has_side_effects=True, vmem_limit_bytes=66 * 1024 * 1024 - 2 * 1024 * 1024
        ),
        name="distill",
    )(th, tgain[None, :], head, sh, sgain[None, :], table, ec, ids[:, None])


def solution(mesh):
    return jax.shard_map(
        per_device,
        mesh=mesh,
        in_specs=(
            P("dp", "vocab"),
            P("vocab"),
            P(("dp", "vocab"), None),
            P("dp", "vocab"),
            P("vocab"),
            P(("dp", "vocab"), None),
            P("dp", "vocab"),
            P("dp"),
        ),
        out_specs=(P("dp", "vocab"), P(("dp", "vocab"), None)),
        check_vma=False,
    )
```

```python
import math

import jax
import jax.numpy as jnp
from jax import lax
from jax.experimental import pallas as pl
from jax.experimental.pallas import tpu as pltpu
from jax.sharding import PartitionSpec as P

MESH = pl.DeviceIdType.MESH
F32, BF16 = jnp.float32, jnp.bfloat16
ORDER = (("z", "x", "y"), ("x", "y", "z"), ("y", "z", "x"))
PARTS = (1, 2, 0)
NT = (((1,), (1,)), ((), ()))
NN = (((1,), (0,)), ((), ()))


def dot(a, b, dims=NN):
    return lax.dot_general(a, b, dims, preferred_element_type=F32)


class Place:
    def __init__(self):
        dp, vocab = lax.axis_index("dp"), lax.axis_index("vocab")
        self.vocab, self.dp = vocab, dp
        self.core = dp % 2
        self.at = {"x": (dp // 8) * 2 + vocab % 2, "y": (dp // 2) % 4, "z": vocab // 2}
        self.x_lo = vocab % 2

    def device(self, core=None, **moved):
        at = {**self.at, **moved}
        core = self.core if core is None else core
        return ((at["x"] // 2) * 8 + at["y"] * 2 + core, at["z"] * 2 + at["x"] % 2)

    def along(self, axis, by):
        return (self.at[axis] + by) % 4

    def shifted(self, axis, by):
        return self.device(**{axis: self.along(axis, by)})

    def sibling(self):
        return self.device(core=1 - self.core)


class Copies:
    def __init__(self, send_sems, recv_sems):
        self.send_sems, self.recv_sems, self.count, self.all = send_sems, recv_sems, 0, []

    def start(self, src, dst, device):
        copy = pltpu.make_async_remote_copy(
            src_ref=src,
            dst_ref=dst,
            send_sem=self.send_sems.at[self.count],
            recv_sem=self.recv_sems.at[self.count],
            device_id=device,
            device_id_type=MESH,
        )
        self.count += 1
        copy.start()
        self.all.append(copy)
        return copy


def region(fixed, core, part, lanes):
    whole = slice(None)
    z, y = fixed.get("z", whole), fixed.get("y", whole)
    x_lo, x_hi = (fixed["x"] % 2, fixed["x"] // 2) if "x" in fixed else (whole, whole)
    return (z, x_lo, x_hi, y, core, pl.ds(16 * part, 16), lanes)


class Gather:
    def __init__(self, here, copies, buf, width):
        self.here, self.copies, self.buf, self.sibling = here, copies, buf, {}
        self.full, self.low, self.high = pl.ds(0, width), pl.ds(0, width // 2), pl.ds(width // 2, width // 2)

    def push(self, p, ph, by, lanes, device):
        here, axis = self.here, ORDER[p][ph]
        fixed = {a: here.at[a] for a in "xyz" if a not in ORDER[p][:ph]}
        fixed[axis] = here.along(axis, by)
        piece = self.buf.at[region(fixed, here.core, p, lanes)]
        return self.copies.start(piece, piece, device)

    def along(self, p, ph, by):
        return self.here.shifted(ORDER[p][ph], by)

    def to_sibling(self, p, by):
        self.sibling[p, by] = self.push(p, 2, by, self.full, self.here.sibling())

    def start_short(self, ph):
        self.short = [self.push(p, ph, 0, self.full, self.along(p, ph, by)) for by in (1, 3, 2) for p in PARTS]

    def wait_short(self):
        for copy in self.short:
            copy.wait_recv()

    def start_long(self):
        self.first = {}
        for right, left in ((self.low, self.high), (self.high, self.low)):
            for p in PARTS:
                self.first.setdefault((p, 1), []).append(self.push(p, 2, 0, right, self.along(p, 2, 1)))
                self.first.setdefault((p, -1), []).append(self.push(p, 2, 0, left, self.along(p, 2, -1)))
        for p in PARTS:
            self.to_sibling(p, 0)

    def forward_long(self):
        self.second = []
        for p in PARTS:
            self.first[p, 1][0].wait_recv()
            self.second.append(self.push(p, 2, -1, self.low, self.along(p, 2, 1)))
            self.first[p, -1][0].wait_recv()
            self.second.append(self.push(p, 2, 1, self.high, self.along(p, 2, -1)))

    def land_long(self):
        for p in PARTS:
            for by in (1, -1):
                self.first[p, by][1].wait_recv()
                self.to_sibling(p, -by)

    def finish_long(self):
        for p, right, left in zip(PARTS, self.second[::2], self.second[1::2]):
            right.wait_recv()
            left.wait_recv()
            self.to_sibling(p, 2)

    def wait_sibling(self, p, *moves):
        for by in moves or (0, -1, 1, 2):
            self.sibling[p, by].wait_recv()

    def steps(self):
        self.start_short(0)
        yield
        self.wait_short()
        self.start_short(1)
        yield
        self.wait_short()
        self.start_long()
        yield
        self.forward_long()
        yield
        self.land_long()
        yield
        self.finish_long()
        yield
        for p in PARTS:
            self.wait_sibling(p)


def scatter(here, copies, p, buf, half, whole, direct, result):
    low, high, full = pl.ds(0, 256), pl.ds(256, 256), pl.ds(0, 512)
    order = ORDER[p][::-1]

    def slab(ph, by, lanes):
        fixed = {a: here.at[a] for a in order[:ph]}
        fixed[order[ph]] = here.along(order[ph], by)
        return region(fixed, here.core, p, lanes)

    right, left = here.shifted(order[0], 1), here.shifted(order[0], -1)
    first = (
        copies.start(buf.at[slab(0, 2, low)], half.at[0], right),
        copies.start(buf.at[slab(0, 2, high)], half.at[1], left),
    )
    yield
    first[0].wait_recv()
    at = slab(0, 1, low)
    buf[at] = (buf[at].astype(F32) + half[0].astype(F32)).astype(BF16)
    second = [copies.start(buf.at[slab(0, 1, full)], whole.at[0], right)]
    first[1].wait_recv()
    at = slab(0, -1, high)
    buf[at] = (buf[at].astype(F32) + half[1].astype(F32)).astype(BF16)
    second.append(copies.start(buf.at[slab(0, -1, full)], whole.at[1], left))
    yield
    for copy in second:
        copy.wait_recv()
    at = slab(0, 0, full)
    buf[at] = (buf[at].astype(F32) + whole[0].astype(F32) + whole[1].astype(F32)).astype(BF16)
    for ph, got in zip((1, 2), direct):
        sent = [
            copies.start(buf.at[slab(ph, by, full)], got.at[by - 1], here.shifted(order[ph], by)) for by in (1, 3, 2)
        ]
        yield
        total = buf[slab(ph, 0, full)].astype(F32)
        for copy in sent:
            copy.wait_recv()
        for i in range(3):
            total = total + got[i].astype(F32)
        if ph == 1:
            buf[slab(ph, 0, full)] = total.astype(BF16)
        else:
            result[pl.ds(16 * p, 16), :] = total


def scatter_shapes():
    sizes = {"x": (2, 2), "y": (4,), "z": (4,)}
    shapes = []
    for order in ORDER:
        left = ["x", "y", "z"]
        for ph, axis in enumerate(order[::-1]):
            left.remove(axis)
            dims = sum((sizes[a] for a in ("z", "x", "y") if a in left), ())
            if ph == 0:
                shapes.append(pltpu.VMEM((2, *dims, 16, 256), BF16))
            shapes.append(pltpu.VMEM((2 if ph == 0 else 3, *dims, 16, 512), BF16))
    return shapes


def totals(here, copies, sent, got):
    groups = (
        [here.device(core=core, x=here.along("x", by)) for core, by in OTHERS(here.core)],
        [here.shifted("y", by) for by in (1, 2, 3)],
        [here.shifted("z", by) for by in (1, 2, 3)],
    )
    slot = 0
    for step, targets in enumerate(groups):
        started = [copies.start(sent.at[step], got.at[slot + i], target) for i, target in enumerate(targets)]
        yield
        total = sent[step]
        for i, copy in enumerate(started):
            copy.wait_recv()
            total = total + got[slot + i]
        slot += len(targets)
        sent[step + 1] = total


def OTHERS(core):
    return [(1 - core, 0)] + [(c, by) for by in (1, 2, 3) for c in (core, 1 - core)]


def column_to_row(column):
    rows, lanes = lax.broadcasted_iota(jnp.int32, (48, 128), 0), lax.broadcasted_iota(jnp.int32, (48, 128), 1)
    return jnp.sum(jnp.where(rows == lanes, column, 0.0), axis=0, keepdims=True)


def row_to_column(row):
    rows, lanes = lax.broadcasted_iota(jnp.int32, (48, 128), 0), lax.broadcasted_iota(jnp.int32, (48, 128), 1)
    return jnp.sum(jnp.where(rows == lanes, row, 0.0), axis=1, keepdims=True)


def vocab_start(here, copies, slots, first_row, second_row):
    rows = lax.broadcasted_iota(jnp.int32, (8, 128), 0)
    slots[here.vocab] = jnp.where(rows == 0, first_row, jnp.where(rows == 1, second_row, 0.0))
    mine = slots.at[here.vocab]
    return [copies.start(mine, mine, (here.dp, (here.vocab + by) % 8)) for by in range(1, 8)]


def vocab_sum(slots, started):
    for copy in started:
        copy.wait_recv()
    total = slots[0]
    for slot in range(1, 8):
        total = total + slots[slot]
    return total


def kernel(
    th_hbm, tgain_hbm, head_hbm, sh_hbm, sgain_hbm, table_hbm, ec_hbm, ids_hbm,
    hidden_grad_ref, table_grad_hbm,
    TH, TGAIN, SH, SGAIN, EC, IDS,
    A, E, R, SB, HEAD, ST, EXPT, STANH, LGT, LG, OHT, GR, MSG, GOT, SQ, INNER, SCALE, TS, TR,
    *rest,
):
    landing, (send_sems, recv_sems, sib_send, sib_recv, load_sems, out_sems) = rest[:12], rest[12:]
    here = Place()
    copies = Copies(send_sems, recv_sems)
    x_lo = here.x_lo
    width = 3584

    barrier = pltpu.get_barrier_semaphore()
    partners = [here.shifted(axis, by) for axis in "yz" for by in (1, 2, 3)]
    partners += [here.device(core=core, x=here.along("x", by)) for core, by in OTHERS(here.core)]
    partners += [(here.dp, here.along("z", by) * 2 + 1 - x_lo) for by in (1, 2, 3)]
    for partner in partners:
        pl.semaphore_signal(barrier, inc=1, device_id=partner, device_id_type=MESH)

    loads = [
        pltpu.make_async_copy(src, dst, load_sems.at[i])
        for i, (src, dst) in enumerate(
            [(th_hbm, TH), (sh_hbm, SH), (tgain_hbm, TGAIN), (sgain_hbm, SGAIN), (ec_hbm, EC), (ids_hbm, IDS),
             (head_hbm, HEAD), (table_hbm, ST)]
        )
    ]
    for load in loads:
        load.start()
    for load in loads[:6]:
        load.wait()

    th, sh, ec = TH[...].astype(F32), SH[...].astype(F32), EC[...].astype(F32)
    tgain, sgain = TGAIN[...].reshape(1, 576).astype(F32), SGAIN[...].reshape(1, 448).astype(F32)
    low = x_lo == 0
    t_part = jnp.sum(th * th, axis=1, keepdims=True)
    s_part = jnp.sum(sh * sh, axis=1, keepdims=True)
    MSG[0:48, :] = jnp.concatenate([jnp.where(low, sh, th[:, :448]), ec[:, :64]], axis=1).astype(BF16)
    gain_row = jnp.concatenate([jnp.where(low, sgain, tgain[:, :448]), jnp.zeros((1, 64), F32)], axis=1)
    MSG[48:64, :] = jnp.broadcast_to(gain_row, (16, 512)).astype(BF16)
    t_row, s_row = column_to_row(t_part), column_to_row(s_part)
    pl.semaphore_wait(barrier, len(partners))
    started = vocab_start(here, copies, SQ, t_row, s_row)
    pair = copies.start(MSG, GOT, (here.dp, here.vocab + 1 - 2 * x_lo))
    sums = vocab_sum(SQ, started)
    t_scale = lax.rsqrt(row_to_column(sums[0:1]) / 4608 + 1e-06)
    s_scale = lax.rsqrt(row_to_column(sums[1:2]) / width + 1e-06)
    SCALE[...] = jnp.broadcast_to(s_scale, (48, 128))
    pair.wait_recv()
    got = GOT[0:48, :].astype(F32)
    got_gain = GOT[48:64, :].astype(F32)[0:1]

    values = jnp.where(
        low,
        jnp.concatenate([th, got[:, :448]], axis=1),
        jnp.concatenate([th[:, 448:], got[:, :448], sh], axis=1),
    )
    gains = jnp.where(
        low,
        jnp.concatenate([tgain, got_gain[:, :448]], axis=1),
        jnp.concatenate([tgain[:, 448:], got_gain[:, :448], sgain], axis=1),
    )
    lanes = lax.broadcasted_iota(jnp.int32, (48, 1024), 1)
    scales = jnp.where(jnp.logical_or(low, lanes < 128), t_scale, s_scale)
    own = (here.at["z"], x_lo, here.at["x"] // 2, here.at["y"], here.core)
    A[own] = (values * scales * gains).astype(BF16)

    states = Gather(here, copies, A, 1024)
    states.start_short(0)

    ids_row = IDS[...].reshape(1, 48).astype(F32)
    ids = row_to_column(jnp.concatenate([ids_row, jnp.zeros((1, 80), F32)], axis=1))
    spot = lax.broadcasted_iota(jnp.int32, (48, 128), 1)
    top = jnp.floor(ids * (1.0 / 4096.0))
    mid = jnp.floor((ids - 4096.0 * top) * (1.0 / 64.0))
    digits = jnp.where(
        spot == 0, top, jnp.where(spot == 1, mid, jnp.where(spot == 2, ids - 4096.0 * top - 64.0 * mid, 0.0))
    )
    E[own] = jnp.where(
        low,
        jnp.concatenate([ec, got[:, 448:]], axis=1),
        jnp.concatenate([ec[:, 64:], digits], axis=1),
    ).astype(BF16)

    states.wait_short()
    states.start_short(1)
    states.wait_short()
    states.start_long()
    loads[6].wait()
    loads[7].wait()

    def part(ref, z, x, p, lo, hi):
        return ref[z, x, :, :, :, 16 * p : 16 * p + 16, lo:hi].reshape(256, hi - lo)

    def half_rows(m):
        return pl.ds(pl.multiple_of(m * 512, 512), 512)

    def squash(p, m, t_raw, s_raw):
        rows = half_rows(m)
        t_value, s_value = jnp.exp(30.0 * jnp.tanh(t_raw * (1.0 / 30.0))), jnp.tanh(s_raw * (1.0 / 30.0))
        EXPT[p, rows, :] = t_value
        STANH[p, rows, :] = s_value
        sums = jnp.where(
            lax.broadcasted_iota(jnp.int32, (8, 256), 0) == 0,
            jnp.sum(t_value, axis=0, keepdims=True),
            jnp.sum(jnp.exp(30.0 * s_value), axis=0, keepdims=True),
        )
        TS[p, 0] = sums if m == 0 else TS[p, 0] + sums

    def block_logits(by, m, last=False):
        z = here.along("z", by)
        rows = half_rows(m)
        t_at, s_at = pl.multiple_of(z * 1152, 128), pl.multiple_of(z * 896, 128)
        t_raw = dot(HEAD[rows, pl.ds(t_at, 1024)], part(A, z, 0, 1, 0, 1024), NT)
        t_raw += dot(HEAD[rows, pl.ds(t_at + 1024, 128)], part(A, z, 1, 1, 0, 128), NT)
        s_raw = dot(ST[rows, pl.ds(s_at, 896)], part(A, z, 1, 1, 128, 1024), NT)
        if by != 0:
            t_raw += EXPT[1, rows, :]
            s_raw += STANH[1, rows, :]
        if last:
            squash(1, m, t_raw, s_raw)
        else:
            EXPT[1, rows, :] = t_raw
            STANH[1, rows, :] = s_raw

    def low_logits(p, m):
        rows = half_rows(m)
        return sum(dot(HEAD[rows, z * 1152 : z * 1152 + 1024], part(A, z, 0, p, 0, 1024), NT) for z in range(4))

    def high_logits(p, m):
        rows = half_rows(m)
        t_raw = dot(
            jnp.concatenate([HEAD[rows, z * 1152 + 1024 : z * 1152 + 1152] for z in range(4)], axis=1),
            jnp.concatenate([part(A, z, 1, p, 0, 128) for z in range(4)], axis=1),
            NT,
        )
        s_raw = dot(
            jnp.concatenate([ST[rows, z * 896 + 768 : z * 896 + 896] for z in range(4)], axis=1),
            jnp.concatenate([part(A, z, 1, p, 896, 1024) for z in range(4)], axis=1),
            NT,
        )
        for z in range(4):
            s_raw += dot(ST[rows, z * 896 : z * 896 + 768], part(A, z, 1, p, 128, 896), NT)
        return t_raw, s_raw

    def part_logits(p, m):
        t_raw, s_raw = high_logits(p, m)
        squash(p, m, t_raw + low_logits(p, m), s_raw)

    def early_logits(p, m):
        rows = half_rows(m)

        @pl.when(low)
        def _():
            EXPT[p, rows, :], STANH[p, rows, :] = high_logits(p, m)

        @pl.when(jnp.logical_not(low))
        def _():
            EXPT[p, rows, :] = low_logits(p, m)

    def late_logits(p, m):
        rows = half_rows(m)

        @pl.when(low)
        def _():
            squash(p, m, EXPT[p, rows, :] + low_logits(p, m), STANH[p, rows, :])

        @pl.when(jnp.logical_not(low))
        def _():
            t_raw, s_raw = high_logits(p, m)
            squash(p, m, EXPT[p, rows, :] + t_raw, s_raw)

    def start_totals(p):
        steps = totals(here, copies, TS.at[p], TR.at[p])
        next(steps)
        return steps

    def finish(steps):
        for _ in steps:
            pass

    cotangents = Gather(here, copies, E, 512).steps()

    states.wait_sibling(1, 0)
    block_logits(0, 0)
    states.forward_long()
    block_logits(0, 1)
    states.land_long()
    states.wait_sibling(1, -1, 1)
    for m in range(2):
        block_logits(-1, m)
        block_logits(1, m)
    states.wait_sibling(2, -1, 1)
    early_logits(2, 0)
    states.finish_long()
    next(cotangents)
    early_logits(2, 1)
    states.wait_sibling(1, 2)
    block_logits(2, 0, True)
    block_logits(2, 1, True)
    totals_of = {1: start_totals(1)}
    states.wait_sibling(2, 0, 2)
    late_logits(2, 0)
    next(cotangents)
    late_logits(2, 1)
    next(totals_of[1])
    totals_of[2] = start_totals(2)
    states.wait_sibling(0)
    part_logits(0, 0)
    next(cotangents)
    next(totals_of[1])
    next(totals_of[2])
    part_logits(0, 1)
    totals_of[0] = start_totals(0)
    next(cotangents)
    finish(totals_of[1])

    def gradient(p):
        inverse = 1.0 / TS[p, 3]
        t_inverse, s_inverse = inverse[0:1], inverse[1:2]

        def step(m, carry):
            rows = pl.ds(pl.multiple_of(m * 256, 256), 256)
            tanh = STANH[p, rows, :]
            grad = (jnp.exp(30.0 * tanh) * s_inverse - EXPT[p, rows, :] * t_inverse) * (1.0 - tanh * tanh)
            LGT[p, rows, :] = grad.astype(BF16)
            LG[p, :, rows] = grad.T.astype(BF16)
            return carry

        lax.fori_loop(0, 4, step, 0)

    def to_sibling(p, z):
        mine = pl.ds(16 * p, 16)
        return pltpu.make_async_remote_copy(
            src_ref=R.at[z, :, :, :, 1 - here.core, mine],
            dst_ref=SB.at[z, :, :, :, mine],
            send_sem=sib_send.at[p * 4 + z],
            recv_sem=sib_recv.at[p * 4 + z],
            device_id=here.sibling(),
            device_id_type=MESH,
        )

    def normed_grad(p, start, stop):
        def step(z, carry):
            for x in range(2):
                for half in range(2):
                    columns = pl.ds(pl.multiple_of(z * 896 + x * 384 + half * 256, 128), 256)
                    found = dot(LG[p], ST[:, columns]).astype(BF16)
                    R[z, x, :, :, :, 16 * p : 16 * p + 16, half * 256 : half * 256 + 256] = found.reshape(
                        2, 4, 2, 16, 256
                    )
            to_sibling(p, z).start()
            return carry

        lax.fori_loop(start, stop, step, 0)

    def start_scatter(p):
        def step(z, carry):
            to_sibling(p, z).wait_recv()
            at = (z, slice(None), slice(None), slice(None), here.core, pl.ds(16 * p, 16))
            mine = R[at].astype(F32) + SB[z, :, :, :, 16 * p : 16 * p + 16].astype(F32)
            R[at] = mine.astype(BF16)
            return carry

        lax.fori_loop(0, 4, step, 0)
        steps = scatter(
            here, copies, p, R, landing[4 * p], landing[4 * p + 1], landing[4 * p + 2 : 4 * p + 4], GR
        )
        next(steps)
        return steps

    gradient(1)
    normed_grad(1, 0, 2)
    next(totals_of[2])
    next(totals_of[0])
    next(cotangents)
    normed_grad(1, 2, 4)
    finish(totals_of[2])
    scatters = {1: start_scatter(1)}
    gradient(2)
    normed_grad(2, 0, 2)
    next(totals_of[0])
    next(cotangents)
    normed_grad(2, 2, 4)
    scatters[2] = start_scatter(2)
    finish(totals_of[0])
    gradient(0)
    normed_grad(0, 0, 2)
    next(scatters[1])
    normed_grad(0, 2, 4)
    scatters[0] = start_scatter(0)
    finish(cotangents)

    spot = lax.broadcasted_iota(jnp.int32, (8, 128), 1)
    weights = jnp.where(spot == 0, 4096.0, jnp.where(spot == 1, 64.0, jnp.where(spot == 2, 1.0, 0.0)))
    first_entry = ((here.dp * 8 + here.vocab) * 1024).astype(F32)

    def one_hot(p):
        token_row = dot(weights.astype(BF16), part(E, 0, 1, p, 384, 512), NT)[0:1] - first_entry

        def step(m, carry):
            rows = pl.ds(pl.multiple_of(m * 256, 256), 256)
            entry = (lax.broadcasted_iota(jnp.int32, (256, 256), 0) + m * 256).astype(F32)
            OHT[p, rows, :] = jnp.where(entry == token_row, 1.0, 0.0).astype(BF16)
            return carry

        lax.fori_loop(0, 4, step, 0)

    for p in PARTS:
        one_hot(p)

    def table_unit(z, x):
        size = 512 - 128 * x
        at = z * 896 + x * 512

        def step(m, carry):
            rows = half_rows(m)
            grads = jnp.concatenate([LGT[p, rows, :] for p in range(3)], axis=1)
            hot = jnp.concatenate([OHT[p, rows, :] for p in range(3)], axis=1)
            normed = jnp.concatenate(
                [part(A, z, 1, p, 128 + 512 * x, 128 + 512 * x + size) for p in range(3)], axis=0
            )
            cots = jnp.concatenate([part(E, z, x, p, 0, size) for p in range(3)], axis=0)
            found = dot(grads, normed) + math.sqrt(width) * dot(hot, cots)
            HEAD[rows, at : at + size] = found.astype(BF16)
            return carry

        lax.fori_loop(0, 2, step, 0)

    polls = {0: (2,), 2: (0,), 3: (1,), 5: (2, 1), 6: (2,), 7: (0,)}
    stores = []
    for unit in range(8):
        z = unit // 2
        table_unit(z, unit % 2)
        if unit % 2:
            columns = pl.ds(z * 896, 896)
            stores.append(
                pltpu.make_async_copy(HEAD.at[:, columns], table_grad_hbm.at[:, columns], out_sems.at[z])
            )
            stores[-1].start()
        for p in polls.get(unit, ()):
            next(scatters[p])
    next(scatters[0])
    for p in (1, 2, 0):
        finish(scatters[p])

    found = GR[...]
    normed_grad = jnp.where(low, found[:, :448], found[:, 64:])
    s_scale = SCALE[:, 0:1]
    normed = (sh * s_scale * sgain).astype(BF16).astype(F32)
    row = column_to_row(jnp.sum(normed_grad * normed, axis=1, keepdims=True))
    inner = row_to_column(vocab_sum(INNER, vocab_start(here, copies, INNER, row, row))[0:1])
    hidden_grad = s_scale * sgain * normed_grad - sh * s_scale * s_scale * inner / width
    hidden_grad_ref[...] = hidden_grad.astype(BF16)

    for copy in copies.all:
        copy.wait_send()
    for p in PARTS:
        for z in range(4):
            to_sibling(p, z).wait_send()
    for store in stores:
        store.wait()


def per_device(th, tgain, head, sh, sgain, table, ec, ids):
    vmem, hbm = pl.BlockSpec(memory_space=pltpu.VMEM), pl.BlockSpec(memory_space=pl.ANY)
    return pl.pallas_call(
        kernel,
        out_shape=(jax.ShapeDtypeStruct(sh.shape, BF16), jax.ShapeDtypeStruct(table.shape, BF16)),
        in_specs=[hbm] * 8,
        out_specs=(vmem, hbm),
        scratch_shapes=[
            *(pltpu.VMEM(small.shape, small.dtype) for small in (th, tgain, sh, sgain, ec, ids)),
            pltpu.VMEM((4, 2, 2, 4, 2, 48, 1024), BF16),
            pltpu.VMEM((4, 2, 2, 4, 2, 48, 512), BF16),
            pltpu.VMEM((4, 2, 2, 4, 2, 48, 512), BF16),
            pltpu.VMEM((4, 2, 2, 4, 48, 512), BF16),
            pltpu.VMEM(head.shape, BF16),
            pltpu.VMEM(table.shape, BF16),
            pltpu.VMEM((3, 1024, 256), F32),
            pltpu.VMEM((3, 1024, 256), F32),
            pltpu.VMEM((3, 1024, 256), BF16),
            pltpu.VMEM((3, 256, 1024), BF16),
            pltpu.VMEM((3, 1024, 256), BF16),
            pltpu.VMEM((48, 512), F32),
            pltpu.VMEM((64, 512), BF16),
            pltpu.VMEM((64, 512), BF16),
            pltpu.VMEM((8, 8, 128), F32),
            pltpu.VMEM((8, 8, 128), F32),
            pltpu.VMEM((48, 128), F32),
            pltpu.VMEM((3, 4, 8, 256), F32),
            pltpu.VMEM((3, 13, 8, 256), F32),
            *scatter_shapes(),
            pltpu.SemaphoreType.DMA((256,)),
            pltpu.SemaphoreType.DMA((256,)),
            pltpu.SemaphoreType.DMA((12,)),
            pltpu.SemaphoreType.DMA((12,)),
            pltpu.SemaphoreType.DMA((8,)),
            pltpu.SemaphoreType.DMA((4,)),
        ],
        compiler_params=pltpu.CompilerParams(
            collective_id=0, has_side_effects=True, vmem_limit_bytes=66 * 1024 * 1024 - 2 * 1024 * 1024
        ),
        name="distill",
    )(th, tgain, head, sh, sgain, table, ec, ids)


def solution(mesh):
    return jax.shard_map(
        per_device,
        mesh=mesh,
        in_specs=(
            P("dp", "vocab"),
            P("vocab"),
            P(("dp", "vocab"), None),
            P("dp", "vocab"),
            P("vocab"),
            P(("dp", "vocab"), None),
            P("dp", "vocab"),
            P("dp"),
        ),
        out_specs=(P("dp", "vocab"), P(("dp", "vocab"), None)),
        check_vma=False,
    )
```

```python
import math

import jax
import jax.numpy as jnp
from jax import lax
from jax.experimental import pallas as pl
from jax.experimental.pallas import tpu as pltpu
from jax.sharding import PartitionSpec as P

MESH = pl.DeviceIdType.MESH
F32, BF16 = jnp.float32, jnp.bfloat16
ORDER = (("z", "x", "y"), ("x", "y", "z"), ("y", "z", "x"))
PARTS = (1, 2, 0)
SENDS, RECEIVES = 64, 174
NT = (((1,), (1,)), ((), ()))
NN = (((1,), (0,)), ((), ()))


def dot(a, b, dims=NN):
    return lax.dot_general(a, b, dims, preferred_element_type=F32)


class Place:
    def __init__(self):
        dp, vocab = lax.axis_index("dp"), lax.axis_index("vocab")
        self.vocab, self.dp = vocab, dp
        self.core = dp % 2
        self.at = {"x": (dp // 8) * 2 + vocab % 2, "y": (dp // 2) % 4, "z": vocab // 2}
        self.x_lo = vocab % 2

    def device(self, core=None, **moved):
        at = {**self.at, **moved}
        core = self.core if core is None else core
        return ((at["x"] // 2) * 8 + at["y"] * 2 + core, at["z"] * 2 + at["x"] % 2)

    def along(self, axis, by):
        return (self.at[axis] + by) % 4

    def shifted(self, axis, by):
        return self.device(**{axis: self.along(axis, by)})

    def sibling(self):
        return self.device(core=1 - self.core)


class Copies:
    def __init__(self, send_sems, recv_sems):
        self.send_sems, self.recv_sems, self.all = send_sems, recv_sems, []

    def start(self, src, dst, device):
        count = len(self.all)
        if count >= SENDS:
            self.all[count - SENDS].wait_send()
        copy = pltpu.make_async_remote_copy(
            src_ref=src,
            dst_ref=dst,
            send_sem=self.send_sems.at[count % SENDS],
            recv_sem=self.recv_sems.at[count],
            device_id=device,
            device_id_type=MESH,
        )
        copy.start()
        self.all.append(copy)
        return copy

    def finish(self):
        assert len(self.all) == RECEIVES, len(self.all)
        for copy in self.all[-SENDS:]:
            copy.wait_send()


def region(fixed, core, part, lanes):
    whole = slice(None)
    z, y = fixed.get("z", whole), fixed.get("y", whole)
    x_lo, x_hi = (fixed["x"] % 2, fixed["x"] // 2) if "x" in fixed else (whole, whole)
    return (z, x_lo, x_hi, y, core, pl.ds(16 * part, 16), lanes)


class Gather:
    def __init__(self, here, copies, buf, width):
        self.here, self.copies, self.buf, self.sibling = here, copies, buf, {}
        self.full, self.low, self.high = pl.ds(0, width), pl.ds(0, width // 2), pl.ds(width // 2, width // 2)

    def push(self, p, ph, by, lanes, device):
        here, axis = self.here, ORDER[p][ph]
        fixed = {a: here.at[a] for a in "xyz" if a not in ORDER[p][:ph]}
        fixed[axis] = here.along(axis, by)
        piece = self.buf.at[region(fixed, here.core, p, lanes)]
        return self.copies.start(piece, piece, device)

    def along(self, p, ph, by):
        return self.here.shifted(ORDER[p][ph], by)

    def to_sibling(self, p, by):
        self.sibling[p, by] = self.push(p, 2, by, self.full, self.here.sibling())

    def start_short(self, ph):
        self.short = [self.push(p, ph, 0, self.full, self.along(p, ph, by)) for by in (1, 3, 2) for p in PARTS]

    def wait_short(self):
        for copy in self.short:
            copy.wait_recv()

    def start_long(self):
        self.first = {
            (p, by): self.push(p, 2, 0, self.full, self.along(p, 2, by)) for p in PARTS for by in (1, -1)
        }
        for p in PARTS:
            self.to_sibling(p, 0)

    def forward_long(self):
        self.second = []
        for p in PARTS:
            self.first[p, 1].wait_recv()
            self.second.append(self.push(p, 2, -1, self.low, self.along(p, 2, 1)))
            self.first[p, -1].wait_recv()
            self.second.append(self.push(p, 2, 1, self.high, self.along(p, 2, -1)))
        for p in PARTS:
            for by in (-1, 1):
                self.to_sibling(p, by)

    def finish_long(self):
        for p, right, left in zip(PARTS, self.second[::2], self.second[1::2]):
            right.wait_recv()
            left.wait_recv()
            self.to_sibling(p, 2)

    def wait_sibling(self, p, *moves):
        for by in moves or (0, -1, 1, 2):
            self.sibling[p, by].wait_recv()


def scatter(here, copies, p, buf, half, whole, direct, result):
    low, high, full = pl.ds(0, 256), pl.ds(256, 256), pl.ds(0, 512)
    order = ORDER[p][::-1]

    def slab(ph, by, lanes):
        fixed = {a: here.at[a] for a in order[:ph]}
        fixed[order[ph]] = here.along(order[ph], by)
        return region(fixed, here.core, p, lanes)

    right, left = here.shifted(order[0], 1), here.shifted(order[0], -1)
    first = (
        copies.start(buf.at[slab(0, 2, low)], half.at[0], right),
        copies.start(buf.at[slab(0, 2, high)], half.at[1], left),
    )
    yield
    first[0].wait_recv()
    at = slab(0, 1, low)
    buf[at] = (buf[at].astype(F32) + half[0].astype(F32)).astype(BF16)
    second = [copies.start(buf.at[slab(0, 1, full)], whole.at[0], right)]
    first[1].wait_recv()
    at = slab(0, -1, high)
    buf[at] = (buf[at].astype(F32) + half[1].astype(F32)).astype(BF16)
    second.append(copies.start(buf.at[slab(0, -1, full)], whole.at[1], left))
    yield
    for copy in second:
        copy.wait_recv()
    at = slab(0, 0, full)
    buf[at] = (buf[at].astype(F32) + whole[0].astype(F32) + whole[1].astype(F32)).astype(BF16)
    for ph, got in zip((1, 2), direct):
        sent = [
            copies.start(buf.at[slab(ph, by, full)], got.at[by - 1], here.shifted(order[ph], by)) for by in (1, 3, 2)
        ]
        yield
        total = buf[slab(ph, 0, full)].astype(F32)
        for copy in sent:
            copy.wait_recv()
        for i in range(3):
            total = total + got[i].astype(F32)
        if ph == 1:
            buf[slab(ph, 0, full)] = total.astype(BF16)
        else:
            result[pl.ds(16 * p, 16), :] = total


def scatter_shapes():
    sizes = {"x": (2, 2), "y": (4,), "z": (4,)}
    shapes = []
    for order in ORDER:
        left = ["x", "y", "z"]
        for ph, axis in enumerate(order[::-1]):
            left.remove(axis)
            dims = sum((sizes[a] for a in ("z", "x", "y") if a in left), ())
            if ph == 0:
                shapes.append(pltpu.VMEM((2, *dims, 16, 256), BF16))
            shapes.append(pltpu.VMEM((2 if ph == 0 else 3, *dims, 16, 512), BF16))
    return shapes


def totals(here, copies, sent, got):
    groups = (
        [here.device(core=core, x=here.along("x", by)) for core, by in OTHERS(here.core)],
        [here.shifted("y", by) for by in (1, 2, 3)],
        [here.shifted("z", by) for by in (1, 2, 3)],
    )
    slot = 0
    for step, targets in enumerate(groups):
        started = [copies.start(sent.at[step], got.at[slot + i], target) for i, target in enumerate(targets)]
        yield
        total = sent[step]
        for i, copy in enumerate(started):
            copy.wait_recv()
            total = total + got[slot + i]
        slot += len(targets)
        sent[step + 1] = total


def OTHERS(core):
    return [(1 - core, 0)] + [(c, by) for by in (1, 2, 3) for c in (core, 1 - core)]


def column_to_row(column):
    rows, lanes = lax.broadcasted_iota(jnp.int32, (48, 128), 0), lax.broadcasted_iota(jnp.int32, (48, 128), 1)
    return jnp.sum(jnp.where(rows == lanes, column, 0.0), axis=0, keepdims=True)


def row_to_column(row):
    rows, lanes = lax.broadcasted_iota(jnp.int32, (48, 128), 0), lax.broadcasted_iota(jnp.int32, (48, 128), 1)
    return jnp.sum(jnp.where(rows == lanes, row, 0.0), axis=1, keepdims=True)


def vocab_start(here, copies, slots, first_row, second_row):
    rows = lax.broadcasted_iota(jnp.int32, (8, 128), 0)
    slots[here.vocab] = jnp.where(rows == 0, first_row, jnp.where(rows == 1, second_row, 0.0))
    mine = slots.at[here.vocab]
    return [copies.start(mine, mine, (here.dp, (here.vocab + by) % 8)) for by in range(1, 8)]


def vocab_sum(slots, started):
    for copy in started:
        copy.wait_recv()
    total = slots[0]
    for slot in range(1, 8):
        total = total + slots[slot]
    return total


def kernel(
    th_hbm, tgain_hbm, head_hbm, sh_hbm, sgain_hbm, table_hbm, ec_hbm, ids_hbm,
    hidden_grad_ref, table_grad_hbm,
    TH, TGAIN, SH, SGAIN, EC, IDS,
    A, E, R, SB, HEAD, ST, EXPT, SRAW, LGT, LG, OHT, GR, MSG, GOT, SQ, SCALE, TS, TR, TI, TIR,
    *rest,
):
    landing, (send_sems, recv_sems, sib_send, sib_recv, load_sems, out_sems) = rest[:12], rest[12:]
    here = Place()
    copies = Copies(send_sems, recv_sems)
    x_lo = here.x_lo
    width = 3584

    barrier = pltpu.get_barrier_semaphore()
    partners = [here.shifted(axis, by) for axis in "yz" for by in (1, 2, 3)]
    partners += [here.device(core=core, x=here.along("x", by)) for core, by in OTHERS(here.core)]
    partners += [(here.dp, here.along("z", by) * 2 + 1 - x_lo) for by in (1, 2, 3)]
    for partner in partners:
        pl.semaphore_signal(barrier, inc=1, device_id=partner, device_id_type=MESH)

    loads = [
        pltpu.make_async_copy(src, dst, load_sems.at[i])
        for i, (src, dst) in enumerate(
            [(th_hbm, TH), (sh_hbm, SH), (tgain_hbm, TGAIN), (sgain_hbm, SGAIN), (ec_hbm, EC), (ids_hbm, IDS),
             (head_hbm, HEAD), (table_hbm, ST)]
        )
    ]
    for load in loads:
        load.start()
    for load in loads[:6]:
        load.wait()

    th, sh, ec = TH[...].astype(F32), SH[...].astype(F32), EC[...].astype(F32)
    tgain, sgain = TGAIN[...].reshape(1, 576).astype(F32), SGAIN[...].reshape(1, 448).astype(F32)
    low = x_lo == 0
    t_part = jnp.sum(th * th, axis=1, keepdims=True)
    s_part = jnp.sum(sh * sh, axis=1, keepdims=True)
    MSG[0:48, :] = jnp.concatenate([jnp.where(low, sh, th[:, :448]), ec[:, :64]], axis=1).astype(BF16)
    gain_row = jnp.concatenate([jnp.where(low, sgain, tgain[:, :448]), jnp.zeros((1, 64), F32)], axis=1)
    MSG[48:64, :] = jnp.broadcast_to(gain_row, (16, 512)).astype(BF16)
    t_row, s_row = column_to_row(t_part), column_to_row(s_part)
    pl.semaphore_wait(barrier, len(partners))
    started = vocab_start(here, copies, SQ, t_row, s_row)
    pair = copies.start(MSG, GOT, (here.dp, here.vocab + 1 - 2 * x_lo))
    sums = vocab_sum(SQ, started)
    t_scale = lax.rsqrt(row_to_column(sums[0:1]) / 4608 + 1e-06)
    s_scale = lax.rsqrt(row_to_column(sums[1:2]) / width + 1e-06)
    SCALE[...] = jnp.broadcast_to(s_scale, (48, 128))
    pair.wait_recv()
    got = GOT[0:48, :].astype(F32)
    got_gain = GOT[48:64, :].astype(F32)[0:1]

    values = jnp.where(
        low,
        jnp.concatenate([th, got[:, :448]], axis=1),
        jnp.concatenate([th[:, 448:], got[:, :448], sh], axis=1),
    )
    gains = jnp.where(
        low,
        jnp.concatenate([tgain, got_gain[:, :448]], axis=1),
        jnp.concatenate([tgain[:, 448:], got_gain[:, :448], sgain], axis=1),
    )
    lanes = lax.broadcasted_iota(jnp.int32, (48, 1024), 1)
    scales = jnp.where(jnp.logical_or(low, lanes < 128), t_scale, s_scale)
    own = (here.at["z"], x_lo, here.at["x"] // 2, here.at["y"], here.core)
    A[own] = (values * scales * gains).astype(BF16)

    states = Gather(here, copies, A, 1024)
    states.start_short(0)

    ids_row = IDS[...].reshape(1, 48).astype(F32)
    ids = row_to_column(jnp.concatenate([ids_row, jnp.zeros((1, 80), F32)], axis=1))
    spot = lax.broadcasted_iota(jnp.int32, (48, 128), 1)
    top = jnp.floor(ids * (1.0 / 4096.0))
    mid = jnp.floor((ids - 4096.0 * top) * (1.0 / 64.0))
    digits = jnp.where(
        spot == 0, top, jnp.where(spot == 1, mid, jnp.where(spot == 2, ids - 4096.0 * top - 64.0 * mid, 0.0))
    )
    E[own] = jnp.where(
        low,
        jnp.concatenate([ec, got[:, 448:]], axis=1),
        jnp.concatenate([ec[:, 64:], digits], axis=1),
    ).astype(BF16)

    cotangents = Gather(here, copies, E, 512)
    cotangents.start_short(0)
    states.wait_short()
    states.start_short(1)
    cotangents.wait_short()
    cotangents.start_short(1)
    states.wait_short()
    states.start_long()
    cotangents.wait_short()
    loads[6].wait()
    loads[7].wait()

    def part(ref, z, x, p, lo, hi):
        return ref[z, x, :, :, :, 16 * p : 16 * p + 16, lo:hi].reshape(256, hi - lo)

    def half_rows(m):
        return pl.ds(pl.multiple_of(m * 512, 512), 512)

    def squash(p, m, t_raw, s_raw):
        rows = half_rows(m)
        t_value = jnp.exp(30.0 * jnp.tanh(t_raw * (1.0 / 30.0)))
        s_value = jnp.exp(30.0 * jnp.tanh(s_raw * (1.0 / 30.0)))
        EXPT[p, rows, :] = t_value
        SRAW[p, rows, :] = s_raw
        sums = jnp.where(
            lax.broadcasted_iota(jnp.int32, (8, 256), 0) == 0,
            jnp.sum(t_value, axis=0, keepdims=True),
            jnp.sum(s_value, axis=0, keepdims=True),
        )
        TS[p, 0] = sums if m == 0 else TS[p, 0] + sums

    def block_logits(by, m, last=False):
        z = here.along("z", by)
        rows = half_rows(m)
        t_at, s_at = pl.multiple_of(z * 1152, 128), pl.multiple_of(z * 896, 128)
        t_raw = dot(HEAD[rows, pl.ds(t_at, 1024)], part(A, z, 0, 1, 0, 1024), NT)
        t_raw += dot(HEAD[rows, pl.ds(t_at + 1024, 128)], part(A, z, 1, 1, 0, 128), NT)
        s_raw = dot(ST[rows, pl.ds(s_at, 896)], part(A, z, 1, 1, 128, 1024), NT)
        if by != 0:
            t_raw += EXPT[1, rows, :]
            s_raw += SRAW[1, rows, :]
        if last:
            squash(1, m, t_raw, s_raw)
        else:
            EXPT[1, rows, :] = t_raw
            SRAW[1, rows, :] = s_raw

    def low_logits(p, m):
        rows = half_rows(m)
        return sum(dot(HEAD[rows, z * 1152 : z * 1152 + 1024], part(A, z, 0, p, 0, 1024), NT) for z in range(4))

    def high_logits(p, m):
        rows = half_rows(m)
        t_raw = dot(
            jnp.concatenate([HEAD[rows, z * 1152 + 1024 : z * 1152 + 1152] for z in range(4)], axis=1),
            jnp.concatenate([part(A, z, 1, p, 0, 128) for z in range(4)], axis=1),
            NT,
        )
        s_raw = dot(
            jnp.concatenate([ST[rows, z * 896 + 768 : z * 896 + 896] for z in range(4)], axis=1),
            jnp.concatenate([part(A, z, 1, p, 896, 1024) for z in range(4)], axis=1),
            NT,
        )
        for z in range(4):
            s_raw += dot(ST[rows, z * 896 : z * 896 + 768], part(A, z, 1, p, 128, 896), NT)
        return t_raw, s_raw

    def part_logits(p, m):
        t_raw, s_raw = high_logits(p, m)
        squash(p, m, t_raw + low_logits(p, m), s_raw)

    def early_logits(p, m):
        rows = half_rows(m)

        @pl.when(low)
        def _():
            EXPT[p, rows, :], SRAW[p, rows, :] = high_logits(p, m)

        @pl.when(jnp.logical_not(low))
        def _():
            EXPT[p, rows, :] = low_logits(p, m)

    def late_logits(p, m):
        rows = half_rows(m)

        @pl.when(low)
        def _():
            squash(p, m, EXPT[p, rows, :] + low_logits(p, m), SRAW[p, rows, :])

        @pl.when(jnp.logical_not(low))
        def _():
            t_raw, s_raw = high_logits(p, m)
            squash(p, m, EXPT[p, rows, :] + t_raw, s_raw)

    def start_totals(p):
        steps = totals(here, copies, TS.at[p], TR.at[p])
        next(steps)
        return steps

    def finish(steps):
        for _ in steps:
            pass

    states.wait_sibling(1, 0)
    for m in range(2):
        block_logits(0, m)
    states.forward_long()
    states.wait_sibling(1, -1, 1)
    for m in range(2):
        block_logits(-1, m)
        block_logits(1, m)
    states.wait_sibling(2, -1, 1)
    early_logits(2, 0)
    early_logits(2, 1)
    states.finish_long()
    cotangents.start_long()
    states.wait_sibling(1, 2)
    block_logits(2, 0, True)
    block_logits(2, 1, True)
    totals_of = {1: start_totals(1)}
    states.wait_sibling(2, 0, 2)
    late_logits(2, 0)
    late_logits(2, 1)
    cotangents.forward_long()
    next(totals_of[1])
    totals_of[2] = start_totals(2)
    states.wait_sibling(0)
    part_logits(0, 0)
    next(totals_of[1])
    next(totals_of[2])
    part_logits(0, 1)
    totals_of[0] = start_totals(0)
    finish(totals_of[1])
    cotangents.finish_long()

    def gradient(p):
        inverse = 1.0 / TS[p, 3]
        t_inverse, s_inverse = inverse[0:1], inverse[1:2]

        def step(m, total):
            rows = pl.ds(pl.multiple_of(m * 256, 256), 256)
            raw = SRAW[p, rows, :]
            tanh = jnp.tanh(raw * (1.0 / 30.0))
            grad = (jnp.exp(30.0 * tanh) * s_inverse - EXPT[p, rows, :] * t_inverse) * (1.0 - tanh * tanh)
            rounded = grad.astype(BF16)
            LGT[p, rows, :] = rounded
            LG[p, :, rows] = grad.T.astype(BF16)
            return total + jnp.sum(rounded.astype(F32) * raw, axis=0, keepdims=True)

        return lax.fori_loop(0, 4, step, jnp.zeros((1, 256), F32))

    def to_sibling(p, z):
        mine = pl.ds(16 * p, 16)
        return pltpu.make_async_remote_copy(
            src_ref=R.at[z, :, :, :, 1 - here.core, mine],
            dst_ref=SB.at[z, :, :, :, mine],
            send_sem=sib_send.at[p * 4 + z],
            recv_sem=sib_recv.at[p * 4 + z],
            device_id=here.sibling(),
            device_id_type=MESH,
        )

    def normed_grad(p, start, stop):
        def step(z, carry):
            for x in range(2):
                for half in range(2):
                    columns = pl.ds(pl.multiple_of(z * 896 + x * 384 + half * 256, 128), 256)
                    found = dot(LG[p], ST[:, columns]).astype(BF16)
                    R[z, x, :, :, :, 16 * p : 16 * p + 16, half * 256 : half * 256 + 256] = found.reshape(
                        2, 4, 2, 16, 256
                    )
            to_sibling(p, z).start()
            return carry

        lax.fori_loop(start, stop, step, 0)

    def start_scatter(p):
        def step(z, carry):
            to_sibling(p, z).wait_recv()
            at = (z, slice(None), slice(None), slice(None), here.core, pl.ds(16 * p, 16))
            mine = R[at].astype(F32) + SB[z, :, :, :, 16 * p : 16 * p + 16].astype(F32)
            R[at] = mine.astype(BF16)
            return carry

        lax.fori_loop(0, 4, step, 0)
        steps = scatter(
            here, copies, p, R, landing[4 * p], landing[4 * p + 1], landing[4 * p + 2 : 4 * p + 4], GR
        )
        next(steps)
        return steps

    inner_parts = {1: gradient(1)}
    normed_grad(1, 0, 2)
    next(totals_of[2])
    next(totals_of[0])
    normed_grad(1, 2, 4)
    finish(totals_of[2])
    scatters = {1: start_scatter(1)}
    inner_parts[2] = gradient(2)
    normed_grad(2, 0, 2)
    next(totals_of[0])
    normed_grad(2, 2, 4)
    scatters[2] = start_scatter(2)
    finish(totals_of[0])
    inner_parts[0] = gradient(0)

    which = lax.broadcasted_iota(jnp.int32, (8, 256), 0)
    TI[0] = jnp.where(which == 0, inner_parts[0], jnp.where(which == 1, inner_parts[1], inner_parts[2]))
    inner_steps = totals(here, copies, TI, TIR)
    next(inner_steps)
    normed_grad(0, 0, 2)
    next(scatters[1])
    next(inner_steps)
    normed_grad(0, 2, 4)
    scatters[0] = start_scatter(0)
    next(inner_steps)
    for p in PARTS:
        cotangents.wait_sibling(p)

    spot = lax.broadcasted_iota(jnp.int32, (8, 128), 1)
    weights = jnp.where(spot == 0, 4096.0, jnp.where(spot == 1, 64.0, jnp.where(spot == 2, 1.0, 0.0)))
    first_entry = ((here.dp * 8 + here.vocab) * 1024).astype(F32)

    def one_hot(p):
        token_row = dot(weights.astype(BF16), part(E, 0, 1, p, 384, 512), NT)[0:1] - first_entry

        def step(m, carry):
            rows = pl.ds(pl.multiple_of(m * 256, 256), 256)
            entry = (lax.broadcasted_iota(jnp.int32, (256, 256), 0) + m * 256).astype(F32)
            OHT[p, rows, :] = jnp.where(entry == token_row, 1.0, 0.0).astype(BF16)
            return carry

        lax.fori_loop(0, 4, step, 0)

    for p in PARTS:
        one_hot(p)

    def table_unit(z, x):
        size = 512 - 128 * x
        at = z * 896 + x * 512

        def step(m, carry):
            rows = half_rows(m)
            grads = jnp.concatenate([LGT[p, rows, :] for p in range(3)], axis=1)
            hot = jnp.concatenate([OHT[p, rows, :] for p in range(3)], axis=1)
            normed = jnp.concatenate(
                [part(A, z, 1, p, 128 + 512 * x, 128 + 512 * x + size) for p in range(3)], axis=0
            )
            cots = jnp.concatenate([part(E, z, x, p, 0, size) for p in range(3)], axis=0)
            found = dot(grads, normed) + math.sqrt(width) * dot(hot, cots)
            HEAD[rows, at : at + size] = found.astype(BF16)
            return carry

        lax.fori_loop(0, 2, step, 0)

    polls = {0: (2,), 1: (0,), 3: (1,), 4: (1, 2), 5: (0, 2), 6: (0,)}
    stores = []
    for unit in range(8):
        z = unit // 2
        table_unit(z, unit % 2)
        if unit % 2:
            columns = pl.ds(z * 896, 896)
            stores.append(
                pltpu.make_async_copy(HEAD.at[:, columns], table_grad_hbm.at[:, columns], out_sems.at[z])
            )
            stores[-1].start()
        for p in polls.get(unit, ()):
            next(scatters[p])
    finish(inner_steps)
    for p in (1, 2, 0):
        finish(scatters[p])

    found = GR[...]
    own_grad = jnp.where(low, found[:, :448], found[:, 64:])
    s_scale = SCALE[:, 0:1]
    lane = lax.broadcasted_iota(jnp.int32, (16, 256), 1) - lax.broadcasted_iota(jnp.int32, (16, 256), 0)
    inner = jnp.concatenate(
        [
            jnp.sum(jnp.where(lane == here.dp * 16, TI[3, p : p + 1, :], 0.0), axis=1, keepdims=True)
            for p in range(3)
        ],
        axis=0,
    )
    hidden_grad = s_scale * sgain * own_grad - sh * s_scale * s_scale * inner / width
    hidden_grad_ref[...] = hidden_grad.astype(BF16)

    copies.finish()
    for p in PARTS:
        for z in range(4):
            to_sibling(p, z).wait_send()
    for store in stores:
        store.wait()


def place_results(hidden_from, table_from, hidden_to, table_to, small, large, in_sems, out_sems):
    rows = table_from.shape[0] // 4
    pieces = [(table_from.at[at], large.at[at], table_to.at[at]) for at in (pl.ds(i * rows, rows) for i in range(4))]
    pieces.append((hidden_from, small, hidden_to))
    ins = [pltpu.make_async_copy(a, b, in_sems.at[i]) for i, (a, b, _) in enumerate(pieces)]
    outs = [pltpu.make_async_copy(b, c, out_sems.at[i]) for i, (_, b, c) in enumerate(pieces)]
    for copy in ins:
        copy.start()
    for copy, out in zip(ins, outs):
        copy.wait()
        out.start()
    for out in outs:
        out.wait()


def per_device(th, tgain, head, sh, sgain, table, ec, ids):
    vmem, hbm = pl.BlockSpec(memory_space=pltpu.VMEM), pl.BlockSpec(memory_space=pl.ANY)
    found = pl.pallas_call(
        kernel,
        out_shape=(jax.ShapeDtypeStruct(sh.shape, BF16), jax.ShapeDtypeStruct(table.shape, BF16)),
        in_specs=[hbm] * 8,
        out_specs=(vmem, hbm),
        scratch_shapes=[
            *(pltpu.VMEM(small.shape, small.dtype) for small in (th, tgain, sh, sgain, ec, ids)),
            pltpu.VMEM((4, 2, 2, 4, 2, 48, 1024), BF16),
            pltpu.VMEM((4, 2, 2, 4, 2, 48, 512), BF16),
            pltpu.VMEM((4, 2, 2, 4, 2, 48, 512), BF16),
            pltpu.VMEM((4, 2, 2, 4, 48, 512), BF16),
            pltpu.VMEM(head.shape, BF16),
            pltpu.VMEM(table.shape, BF16),
            pltpu.VMEM((3, 1024, 256), F32),
            pltpu.VMEM((3, 1024, 256), F32),
            pltpu.VMEM((3, 1024, 256), BF16),
            pltpu.VMEM((3, 256, 1024), BF16),
            pltpu.VMEM((3, 1024, 256), BF16),
            pltpu.VMEM((48, 512), F32),
            pltpu.VMEM((64, 512), BF16),
            pltpu.VMEM((64, 512), BF16),
            pltpu.VMEM((8, 8, 128), F32),
            pltpu.VMEM((48, 128), F32),
            pltpu.VMEM((3, 4, 8, 256), F32),
            pltpu.VMEM((3, 13, 8, 256), F32),
            pltpu.VMEM((4, 8, 256), F32),
            pltpu.VMEM((13, 8, 256), F32),
            *scatter_shapes(),
            pltpu.SemaphoreType.DMA((SENDS,)),
            pltpu.SemaphoreType.DMA((RECEIVES,)),
            pltpu.SemaphoreType.DMA((12,)),
            pltpu.SemaphoreType.DMA((12,)),
            pltpu.SemaphoreType.DMA((8,)),
            pltpu.SemaphoreType.DMA((4,)),
        ],
        compiler_params=pltpu.CompilerParams(
            collective_id=0, has_side_effects=True, vmem_limit_bytes=66 * 1024 * 1024 - 2 * 1024 * 1024
        ),
        name="distill",
    )(th, tgain, head, sh, sgain, table, ec, ids)
    return pl.pallas_call(
        place_results,
        out_shape=tuple(jax.ShapeDtypeStruct(a.shape, a.dtype) for a in found),
        in_specs=[hbm] * 2,
        out_specs=(hbm, hbm),
        scratch_shapes=[
            pltpu.VMEM(sh.shape, BF16),
            pltpu.VMEM(table.shape, BF16),
            pltpu.SemaphoreType.DMA((5,)),
            pltpu.SemaphoreType.DMA((5,)),
        ],
        compiler_params=pltpu.CompilerParams(vmem_limit_bytes=64 * 1024 * 1024),
        name="place",
    )(*found)


def solution(mesh):
    return jax.shard_map(
        per_device,
        mesh=mesh,
        in_specs=(
            P("dp", "vocab"),
            P("vocab"),
            P(("dp", "vocab"), None),
            P("dp", "vocab"),
            P("vocab"),
            P(("dp", "vocab"), None),
            P("dp", "vocab"),
            P("dp"),
        ),
        out_specs=(P("dp", "vocab"), P(("dp", "vocab"), None)),
        check_vma=False,
    )
```

```python
import math

import jax
import jax.numpy as jnp
from jax import lax
from jax.experimental import pallas as pl
from jax.experimental.pallas import tpu as pltpu
from jax.sharding import PartitionSpec as P

MESH = pl.DeviceIdType.MESH
F32, BF16 = jnp.float32, jnp.bfloat16
ORDER = (("z", "x", "y"), ("x", "y", "z"), ("y", "z", "x"))
PARTS = (1, 2, 0)
SENDS, RECEIVES = 64, 181
NT = (((1,), (1,)), ((), ()))
NN = (((1,), (0,)), ((), ()))


def dot(a, b, dims=NN):
    return lax.dot_general(a, b, dims, preferred_element_type=F32)


class Place:
    def __init__(self):
        dp, vocab = lax.axis_index("dp"), lax.axis_index("vocab")
        self.vocab, self.dp = vocab, dp
        self.core = dp % 2
        self.at = {"x": (dp // 8) * 2 + vocab % 2, "y": (dp // 2) % 4, "z": vocab // 2}
        self.x_lo = vocab % 2

    def device(self, core=None, **moved):
        at = {**self.at, **moved}
        core = self.core if core is None else core
        return ((at["x"] // 2) * 8 + at["y"] * 2 + core, at["z"] * 2 + at["x"] % 2)

    def along(self, axis, by):
        return (self.at[axis] + by) % 4

    def shifted(self, axis, by):
        return self.device(**{axis: self.along(axis, by)})

    def sibling(self):
        return self.device(core=1 - self.core)


class Copies:
    def __init__(self, send_sems, recv_sems):
        self.send_sems, self.recv_sems, self.all = send_sems, recv_sems, []

    def start(self, src, dst, device):
        count = len(self.all)
        if count >= SENDS:
            self.all[count - SENDS].wait_send()
        copy = pltpu.make_async_remote_copy(
            src_ref=src,
            dst_ref=dst,
            send_sem=self.send_sems.at[count % SENDS],
            recv_sem=self.recv_sems.at[count],
            device_id=device,
            device_id_type=MESH,
        )
        copy.start()
        self.all.append(copy)
        return copy

    def finish(self):
        assert len(self.all) == RECEIVES, len(self.all)
        for copy in self.all[-SENDS:]:
            copy.wait_send()


def region(fixed, core, part, lanes):
    whole = slice(None)
    z, y = fixed.get("z", whole), fixed.get("y", whole)
    x_lo, x_hi = (fixed["x"] % 2, fixed["x"] // 2) if "x" in fixed else (whole, whole)
    return (z, x_lo, x_hi, y, core, pl.ds(16 * part, 16), lanes)


class Gather:
    def __init__(self, here, copies, buf, width):
        self.here, self.copies, self.buf, self.sibling = here, copies, buf, {}
        self.full, self.low, self.high = pl.ds(0, width), pl.ds(0, width // 2), pl.ds(width // 2, width // 2)

    def push(self, p, ph, by, lanes, device):
        here, axis = self.here, ORDER[p][ph]
        fixed = {a: here.at[a] for a in "xyz" if a not in ORDER[p][:ph]}
        fixed[axis] = here.along(axis, by)
        piece = self.buf.at[region(fixed, here.core, p, lanes)]
        return self.copies.start(piece, piece, device)

    def along(self, p, ph, by):
        return self.here.shifted(ORDER[p][ph], by)

    def to_sibling(self, p, by):
        self.sibling[p, by] = self.push(p, 2, by, self.full, self.here.sibling())

    def start_short(self, ph):
        self.short = [self.push(p, ph, 0, self.full, self.along(p, ph, by)) for by in (1, 3, 2) for p in PARTS]

    def wait_short(self):
        for copy in self.short:
            copy.wait_recv()

    def start_long(self):
        self.first = {
            (p, by): self.push(p, 2, 0, self.full, self.along(p, 2, by)) for p in PARTS for by in (1, -1)
        }
        for p in PARTS:
            self.to_sibling(p, 0)

    def start_direct(self):
        self.first = {
            (p, by): self.push(p, 2, 0, self.full, self.along(p, 2, by)) for by in (1, -1, 2) for p in PARTS
        }

    def finish_direct(self):
        for p in PARTS:
            for by in (1, -1, 2):
                self.first[p, by].wait_recv()
                self.to_sibling(p, -by if by != 2 else 2)

    def forward_long(self):
        self.second = []
        for p in PARTS:
            self.first[p, 1].wait_recv()
            self.second.append(self.push(p, 2, -1, self.low, self.along(p, 2, 1)))
            self.first[p, -1].wait_recv()
            self.second.append(self.push(p, 2, 1, self.high, self.along(p, 2, -1)))
        for p in PARTS:
            for by in (-1, 1):
                self.to_sibling(p, by)

    def finish_long(self):
        for p, right, left in zip(PARTS, self.second[::2], self.second[1::2]):
            right.wait_recv()
            left.wait_recv()
            self.to_sibling(p, 2)

    def wait_sibling(self, p, *moves):
        for by in moves or (0, -1, 1, 2):
            self.sibling[p, by].wait_recv()


SCATTERS = {
    "1": (1, ("z", "y", "x"), 0, 512),
    "2": (2, ("x", "z", "y"), 0, 512),
    "0a": (0, ("y", "x", "z"), 0, 256),
    "0b": (0, ("z", "x", "y"), 256, 256),
}


def scatter(here, copies, p, order, start, width, buf, landing, result):
    half, whole, *direct = landing
    low, high, full = pl.ds(start, width // 2), pl.ds(start + width // 2, width // 2), pl.ds(start, width)

    def slab(ph, by, lanes):
        fixed = {a: here.at[a] for a in order[:ph]}
        fixed[order[ph]] = here.along(order[ph], by)
        return region(fixed, here.core, p, lanes)

    right, left = here.shifted(order[0], 1), here.shifted(order[0], -1)
    first = (
        copies.start(buf.at[slab(0, 2, low)], half.at[0], right),
        copies.start(buf.at[slab(0, 2, high)], half.at[1], left),
    )
    yield
    first[0].wait_recv()
    at = slab(0, 1, low)
    buf[at] = (buf[at].astype(F32) + half[0].astype(F32)).astype(BF16)
    second = [copies.start(buf.at[slab(0, 1, full)], whole.at[0], right)]
    first[1].wait_recv()
    at = slab(0, -1, high)
    buf[at] = (buf[at].astype(F32) + half[1].astype(F32)).astype(BF16)
    second.append(copies.start(buf.at[slab(0, -1, full)], whole.at[1], left))
    yield
    for copy in second:
        copy.wait_recv()
    at = slab(0, 0, full)
    buf[at] = (buf[at].astype(F32) + whole[0].astype(F32) + whole[1].astype(F32)).astype(BF16)
    for ph, got in zip((1, 2), direct):
        sent = [
            copies.start(buf.at[slab(ph, by, full)], got.at[by - 1], here.shifted(order[ph], by)) for by in (1, 3, 2)
        ]
        yield
        total = buf[slab(ph, 0, full)].astype(F32)
        for copy in sent:
            copy.wait_recv()
        for i in range(3):
            total = total + got[i].astype(F32)
        if ph == 1:
            buf[slab(ph, 0, full)] = total.astype(BF16)
        else:
            result[pl.ds(16 * p, 16), full] = total


def scatter_shapes():
    sizes = {"x": (2, 2), "y": (4,), "z": (4,)}
    shapes = []
    for _, order, _, width in SCATTERS.values():
        for ph in range(3):
            dims = sum((sizes[a] for a in ("z", "x", "y") if a in order[ph + 1 :]), ())
            if ph == 0:
                shapes.append(pltpu.VMEM((2, *dims, 16, width // 2), BF16))
            shapes.append(pltpu.VMEM((2 if ph == 0 else 3, *dims, 16, width), BF16))
    return shapes


def totals(here, copies, sent, got):
    groups = (
        [here.device(core=core, x=here.along("x", by)) for core, by in OTHERS(here.core)],
        [here.shifted("y", by) for by in (1, 2, 3)],
        [here.shifted("z", by) for by in (1, 2, 3)],
    )
    slot = 0
    for step, targets in enumerate(groups):
        started = [copies.start(sent.at[step], got.at[slot + i], target) for i, target in enumerate(targets)]
        yield
        total = sent[step]
        for i, copy in enumerate(started):
            copy.wait_recv()
            total = total + got[slot + i]
        slot += len(targets)
        sent[step + 1] = total


def OTHERS(core):
    return [(1 - core, 0)] + [(c, by) for by in (1, 2, 3) for c in (core, 1 - core)]


def column_to_row(column):
    rows, lanes = lax.broadcasted_iota(jnp.int32, (48, 128), 0), lax.broadcasted_iota(jnp.int32, (48, 128), 1)
    return jnp.sum(jnp.where(rows == lanes, column, 0.0), axis=0, keepdims=True)


def row_to_column(row):
    rows, lanes = lax.broadcasted_iota(jnp.int32, (48, 128), 0), lax.broadcasted_iota(jnp.int32, (48, 128), 1)
    return jnp.sum(jnp.where(rows == lanes, row, 0.0), axis=1, keepdims=True)


def vocab_start(here, copies, slots, first_row, second_row):
    rows = lax.broadcasted_iota(jnp.int32, (8, 128), 0)
    slots[here.vocab] = jnp.where(rows == 0, first_row, jnp.where(rows == 1, second_row, 0.0))
    mine = slots.at[here.vocab]
    return [copies.start(mine, mine, (here.dp, (here.vocab + by) % 8)) for by in range(1, 8)]


def vocab_sum(slots, started):
    for copy in started:
        copy.wait_recv()
    total = slots[0]
    for slot in range(1, 8):
        total = total + slots[slot]
    return total


def kernel(
    th_hbm, tgain_hbm, head_hbm, sh_hbm, sgain_hbm, table_hbm, ec_hbm, ids_hbm,
    hidden_grad_ref, HEAD,
    TH, TGAIN, SH, SGAIN, EC, IDS,
    A, E, R, SB, ST, EXPT, SRAW, LGT, LG, OHT, GR, MSG, GOT, SQ, SCALE, TS, TR, TI, TIR,
    *rest,
):
    landing, (send_sems, recv_sems, sib_send, sib_recv, load_sems) = rest[:16], rest[16:]
    here = Place()
    copies = Copies(send_sems, recv_sems)
    x_lo = here.x_lo
    width = 3584

    barrier = pltpu.get_barrier_semaphore()
    partners = [here.shifted(axis, by) for axis in "yz" for by in (1, 2, 3)]
    partners += [here.device(core=core, x=here.along("x", by)) for core, by in OTHERS(here.core)]
    partners += [(here.dp, here.along("z", by) * 2 + 1 - x_lo) for by in (1, 2, 3)]
    for partner in partners:
        pl.semaphore_signal(barrier, inc=1, device_id=partner, device_id_type=MESH)

    loads = [
        pltpu.make_async_copy(src, dst, load_sems.at[i])
        for i, (src, dst) in enumerate(
            [(th_hbm, TH), (sh_hbm, SH), (tgain_hbm, TGAIN), (sgain_hbm, SGAIN), (ec_hbm, EC), (ids_hbm, IDS),
             (head_hbm, HEAD), (table_hbm, ST)]
        )
    ]
    for load in loads:
        load.start()
    for load in loads[:6]:
        load.wait()

    th, sh, ec = TH[...].astype(F32), SH[...].astype(F32), EC[...].astype(F32)
    tgain, sgain = TGAIN[...].reshape(1, 576).astype(F32), SGAIN[...].reshape(1, 448).astype(F32)
    low = x_lo == 0
    t_part = jnp.sum(th * th, axis=1, keepdims=True)
    s_part = jnp.sum(sh * sh, axis=1, keepdims=True)
    MSG[0:48, :] = jnp.concatenate([jnp.where(low, sh, th[:, :448]), ec[:, :64]], axis=1).astype(BF16)
    gain_row = jnp.concatenate([jnp.where(low, sgain, tgain[:, :448]), jnp.zeros((1, 64), F32)], axis=1)
    MSG[48:64, :] = jnp.broadcast_to(gain_row, (16, 512)).astype(BF16)
    t_row, s_row = column_to_row(t_part), column_to_row(s_part)
    pl.semaphore_wait(barrier, len(partners))
    started = vocab_start(here, copies, SQ, t_row, s_row)
    pair = copies.start(MSG, GOT, (here.dp, here.vocab + 1 - 2 * x_lo))
    sums = vocab_sum(SQ, started)
    t_scale = lax.rsqrt(row_to_column(sums[0:1]) / 4608 + 1e-06)
    s_scale = lax.rsqrt(row_to_column(sums[1:2]) / width + 1e-06)
    SCALE[...] = jnp.broadcast_to(s_scale, (48, 128))
    pair.wait_recv()
    got = GOT[0:48, :].astype(F32)
    got_gain = GOT[48:64, :].astype(F32)[0:1]

    values = jnp.where(
        low,
        jnp.concatenate([th, got[:, :448]], axis=1),
        jnp.concatenate([th[:, 448:], got[:, :448], sh], axis=1),
    )
    gains = jnp.where(
        low,
        jnp.concatenate([tgain, got_gain[:, :448]], axis=1),
        jnp.concatenate([tgain[:, 448:], got_gain[:, :448], sgain], axis=1),
    )
    lanes = lax.broadcasted_iota(jnp.int32, (48, 1024), 1)
    scales = jnp.where(jnp.logical_or(low, lanes < 128), t_scale, s_scale)
    own = (here.at["z"], x_lo, here.at["x"] // 2, here.at["y"], here.core)
    A[own] = (values * scales * gains).astype(BF16)

    states = Gather(here, copies, A, 1024)
    states.start_short(0)

    ids_row = IDS[...].reshape(1, 48).astype(F32)
    ids = row_to_column(jnp.concatenate([ids_row, jnp.zeros((1, 80), F32)], axis=1))
    spot = lax.broadcasted_iota(jnp.int32, (48, 128), 1)
    top = jnp.floor(ids * (1.0 / 4096.0))
    mid = jnp.floor((ids - 4096.0 * top) * (1.0 / 64.0))
    digits = jnp.where(
        spot == 0, top, jnp.where(spot == 1, mid, jnp.where(spot == 2, ids - 4096.0 * top - 64.0 * mid, 0.0))
    )
    E[own] = jnp.where(
        low,
        jnp.concatenate([ec, got[:, 448:]], axis=1),
        jnp.concatenate([ec[:, 64:], digits], axis=1),
    ).astype(BF16)

    cotangents = Gather(here, copies, E, 512)
    cotangents.start_short(0)
    states.wait_short()
    states.start_short(1)
    cotangents.wait_short()
    cotangents.start_short(1)
    states.wait_short()
    states.start_long()
    cotangents.wait_short()
    loads[6].wait()
    loads[7].wait()

    def part(ref, z, x, p, lo, hi):
        return ref[z, x, :, :, :, 16 * p : 16 * p + 16, lo:hi].reshape(256, hi - lo)

    def half_rows(m):
        return pl.ds(pl.multiple_of(m * 512, 512), 512)

    def squash(p, m, t_raw, s_raw):
        rows = half_rows(m)
        t_value = jnp.exp(30.0 * jnp.tanh(t_raw * (1.0 / 30.0)))
        s_value = jnp.exp(30.0 * jnp.tanh(s_raw * (1.0 / 30.0)))
        EXPT[p, rows, :] = t_value
        SRAW[p, rows, :] = s_raw
        sums = jnp.where(
            lax.broadcasted_iota(jnp.int32, (8, 256), 0) == 0,
            jnp.sum(t_value, axis=0, keepdims=True),
            jnp.sum(s_value, axis=0, keepdims=True),
        )
        TS[p, 0] = sums if m == 0 else TS[p, 0] + sums

    def block_logits(by, m, last=False):
        z = here.along("z", by)
        rows = half_rows(m)
        t_at, s_at = pl.multiple_of(z * 1152, 128), pl.multiple_of(z * 896, 128)
        t_raw = dot(HEAD[rows, pl.ds(t_at, 1024)], part(A, z, 0, 1, 0, 1024), NT)
        t_raw += dot(HEAD[rows, pl.ds(t_at + 1024, 128)], part(A, z, 1, 1, 0, 128), NT)
        s_raw = dot(ST[rows, pl.ds(s_at, 896)], part(A, z, 1, 1, 128, 1024), NT)
        if by != 0:
            t_raw += EXPT[1, rows, :]
            s_raw += SRAW[1, rows, :]
        if last:
            squash(1, m, t_raw, s_raw)
        else:
            EXPT[1, rows, :] = t_raw
            SRAW[1, rows, :] = s_raw

    def low_logits(p, m):
        rows = half_rows(m)
        return sum(dot(HEAD[rows, z * 1152 : z * 1152 + 1024], part(A, z, 0, p, 0, 1024), NT) for z in range(4))

    def high_logits(p, m):
        rows = half_rows(m)
        t_raw = dot(
            jnp.concatenate([HEAD[rows, z * 1152 + 1024 : z * 1152 + 1152] for z in range(4)], axis=1),
            jnp.concatenate([part(A, z, 1, p, 0, 128) for z in range(4)], axis=1),
            NT,
        )
        s_raw = dot(
            jnp.concatenate([ST[rows, z * 896 + 768 : z * 896 + 896] for z in range(4)], axis=1),
            jnp.concatenate([part(A, z, 1, p, 896, 1024) for z in range(4)], axis=1),
            NT,
        )
        for z in range(4):
            s_raw += dot(ST[rows, z * 896 : z * 896 + 768], part(A, z, 1, p, 128, 896), NT)
        return t_raw, s_raw

    def part_logits(p, m):
        t_raw, s_raw = high_logits(p, m)
        squash(p, m, t_raw + low_logits(p, m), s_raw)

    def early_logits(p, m):
        rows = half_rows(m)

        @pl.when(low)
        def _():
            EXPT[p, rows, :], SRAW[p, rows, :] = high_logits(p, m)

        @pl.when(jnp.logical_not(low))
        def _():
            EXPT[p, rows, :] = low_logits(p, m)

    def late_logits(p, m):
        rows = half_rows(m)

        @pl.when(low)
        def _():
            squash(p, m, EXPT[p, rows, :] + low_logits(p, m), SRAW[p, rows, :])

        @pl.when(jnp.logical_not(low))
        def _():
            t_raw, s_raw = high_logits(p, m)
            squash(p, m, EXPT[p, rows, :] + t_raw, s_raw)

    def start_totals(p):
        steps = totals(here, copies, TS.at[p], TR.at[p])
        next(steps)
        return steps

    def finish(steps):
        for _ in steps:
            pass

    states.wait_sibling(1, 0)
    for m in range(2):
        block_logits(0, m)
    states.forward_long()
    states.wait_sibling(1, -1, 1)
    for m in range(2):
        block_logits(-1, m)
        block_logits(1, m)
    states.wait_sibling(2, -1, 1)
    early_logits(2, 0)
    early_logits(2, 1)
    states.finish_long()
    cotangents.start_direct()
    states.wait_sibling(1, 2)
    block_logits(2, 0, True)
    block_logits(2, 1, True)
    totals_of = {1: start_totals(1)}
    states.wait_sibling(2, 0, 2)
    late_logits(2, 0)
    late_logits(2, 1)
    next(totals_of[1])
    totals_of[2] = start_totals(2)
    states.wait_sibling(0)
    part_logits(0, 0)
    for p in PARTS:
        cotangents.to_sibling(p, 0)
    next(totals_of[1])
    next(totals_of[2])
    part_logits(0, 1)
    totals_of[0] = start_totals(0)
    finish(totals_of[1])
    cotangents.finish_direct()

    def gradient(p):
        inverse = 1.0 / TS[p, 3]
        t_inverse, s_inverse = inverse[0:1], inverse[1:2]

        def step(m, total):
            rows = pl.ds(pl.multiple_of(m * 256, 256), 256)
            raw = SRAW[p, rows, :]
            tanh = jnp.tanh(raw * (1.0 / 30.0))
            grad = (jnp.exp(30.0 * tanh) * s_inverse - EXPT[p, rows, :] * t_inverse) * (1.0 - tanh * tanh)
            rounded = grad.astype(BF16)
            LGT[p, rows, :] = rounded
            LG[p, :, rows] = grad.T.astype(BF16)
            return total + jnp.sum(rounded.astype(F32) * raw, axis=0, keepdims=True)

        return lax.fori_loop(0, 4, step, jnp.zeros((1, 256), F32))

    def to_sibling(p, z):
        mine = pl.ds(16 * p, 16)
        return pltpu.make_async_remote_copy(
            src_ref=R.at[z, :, :, :, 1 - here.core, mine],
            dst_ref=SB.at[z, :, :, :, mine],
            send_sem=sib_send.at[p * 4 + z],
            recv_sem=sib_recv.at[p * 4 + z],
            device_id=here.sibling(),
            device_id_type=MESH,
        )

    def normed_grad(p, start, stop):
        def step(z, carry):
            for x in range(2):
                for half in range(2):
                    normed_block(p, z, x, half)
            to_sibling(p, z).start()
            return carry

        lax.fori_loop(start, stop, step, 0)

    def normed_block(p, z, x, half):
        columns = pl.ds(pl.multiple_of(z * 896 + x * 384 + half * 256, 128), 256)
        found = dot(LG[p], ST[:, columns]).astype(BF16)
        R[z, x, :, :, :, 16 * p : 16 * p + 16, half * 256 : half * 256 + 256] = found.reshape(2, 4, 2, 16, 256)

    def half_to_sibling(half, pair):
        at, mine, lanes = pl.ds(2 * pair, 2), pl.ds(0, 16), pl.ds(256 * half, 256)
        return pltpu.make_async_remote_copy(
            src_ref=R.at[at, :, :, :, 1 - here.core, mine, lanes],
            dst_ref=SB.at[at, :, :, :, mine, lanes],
            send_sem=sib_send.at[half * 2 + pair],
            recv_sem=sib_recv.at[half * 2 + pair],
            device_id=here.sibling(),
            device_id_type=MESH,
        )

    def normed_grad_half(half):
        for pair in range(2):

            def step(z, carry):
                for x in range(2):
                    normed_block(0, z, x, half)
                return carry

            lax.fori_loop(2 * pair, 2 * pair + 2, step, 0)
            half_to_sibling(half, pair).start()

    def add_sibling(p, z, lanes):
        at = (z, slice(None), slice(None), slice(None), here.core, pl.ds(16 * p, 16), lanes)
        mine = R[at].astype(F32) + SB[z, :, :, :, 16 * p : 16 * p + 16, lanes].astype(F32)
        R[at] = mine.astype(BF16)

    def start_steps(name):
        i = 4 * list(SCATTERS).index(name)
        steps = scatter(here, copies, *SCATTERS[name], R, landing[i : i + 4], GR)
        next(steps)
        return steps

    def start_scatter(p):
        def step(z, carry):
            to_sibling(p, z).wait_recv()
            add_sibling(p, z, pl.ds(0, 512))
            return carry

        lax.fori_loop(0, 4, step, 0)
        return start_steps(str(p))

    def start_scatter_half(half):
        for pair in range(2):
            half_to_sibling(half, pair).wait_recv()

            def step(z, carry):
                add_sibling(0, z, pl.ds(256 * half, 256))
                return carry

            lax.fori_loop(2 * pair, 2 * pair + 2, step, 0)
        return start_steps("0ab"[0] + "ab"[half])

    inner_parts = {1: gradient(1)}
    normed_grad(1, 0, 2)
    next(totals_of[2])
    next(totals_of[0])
    normed_grad(1, 2, 4)
    finish(totals_of[2])
    scatters = {1: start_scatter(1)}
    inner_parts[2] = gradient(2)
    normed_grad(2, 0, 2)
    next(totals_of[0])
    normed_grad(2, 2, 4)
    scatters[2] = start_scatter(2)
    finish(totals_of[0])
    inner_parts[0] = gradient(0)

    which = lax.broadcasted_iota(jnp.int32, (8, 256), 0)
    TI[0] = jnp.where(which == 0, inner_parts[0], jnp.where(which == 1, inner_parts[1], inner_parts[2]))
    inner_steps = totals(here, copies, TI, TIR)
    next(inner_steps)
    normed_grad_half(0)
    next(scatters[1])
    next(inner_steps)
    scatters["a"] = start_scatter_half(0)
    normed_grad_half(1)
    scatters["b"] = start_scatter_half(1)
    next(inner_steps)
    next(scatters[2])
    for p in PARTS:
        cotangents.wait_sibling(p)

    spot = lax.broadcasted_iota(jnp.int32, (8, 128), 1)
    weights = jnp.where(spot == 0, 4096.0, jnp.where(spot == 1, 64.0, jnp.where(spot == 2, 1.0, 0.0)))
    first_entry = ((here.dp * 8 + here.vocab) * 1024).astype(F32)

    def one_hot(p):
        token_row = dot(weights.astype(BF16), part(E, 0, 1, p, 384, 512), NT)[0:1] - first_entry

        def step(m, carry):
            rows = pl.ds(pl.multiple_of(m * 256, 256), 256)
            entry = (lax.broadcasted_iota(jnp.int32, (256, 256), 0) + m * 256).astype(F32)
            OHT[p, rows, :] = jnp.where(entry == token_row, 1.0, 0.0).astype(BF16)
            return carry

        lax.fori_loop(0, 4, step, 0)

    for p in PARTS:
        one_hot(p)

    def table_unit(z, x):
        size = 512 - 128 * x
        at = z * 896 + x * 512

        def step(m, carry):
            rows = half_rows(m)
            grads = jnp.concatenate([LGT[p, rows, :] for p in range(3)], axis=1)
            hot = jnp.concatenate([OHT[p, rows, :] for p in range(3)], axis=1)
            normed = jnp.concatenate(
                [part(A, z, 1, p, 128 + 512 * x, 128 + 512 * x + size) for p in range(3)], axis=0
            )
            cots = jnp.concatenate([part(E, z, x, p, 0, size) for p in range(3)], axis=0)
            found = dot(grads, normed) + math.sqrt(width) * dot(hot, cots)
            HEAD[rows, at : at + size] = found.astype(BF16)
            return carry

        lax.fori_loop(0, 2, step, 0)

    polls = {0: ("a",), 1: ("b",), 2: (1,), 3: ("a", 1), 4: ("b", 2), 5: (2,), 6: ("a",), 7: ("b",)}
    for unit in range(8):
        table_unit(unit // 2, unit % 2)
        for p in polls.get(unit, ()):
            next(scatters[p])
    finish(inner_steps)
    for name in (1, 2, "a", "b"):
        finish(scatters[name])

    found = GR[...]
    own_grad = jnp.where(low, found[:, :448], found[:, 64:])
    s_scale = SCALE[:, 0:1]
    lane = lax.broadcasted_iota(jnp.int32, (16, 256), 1) - lax.broadcasted_iota(jnp.int32, (16, 256), 0)
    inner = jnp.concatenate(
        [
            jnp.sum(jnp.where(lane == here.dp * 16, TI[3, p : p + 1, :], 0.0), axis=1, keepdims=True)
            for p in range(3)
        ],
        axis=0,
    )
    hidden_grad = s_scale * sgain * own_grad - sh * s_scale * s_scale * inner / width
    hidden_grad_ref[...] = hidden_grad.astype(BF16)

    copies.finish()
    for p in (1, 2):
        for z in range(4):
            to_sibling(p, z).wait_send()
    for half in range(2):
        for pair in range(2):
            half_to_sibling(half, pair).wait_send()


def place_results(hidden_from, table_from, hidden_to, table_to, out_sems):
    rows = table_from.shape[0] // 4
    columns = pl.ds(0, table_to.shape[1])
    pieces = [(table_from.at[at, columns], table_to.at[at]) for at in (pl.ds(i * rows, rows) for i in range(4))]
    pieces.append((hidden_from, hidden_to))
    outs = [pltpu.make_async_copy(a, b, out_sems.at[i]) for i, (a, b) in enumerate(pieces)]
    for out in outs:
        out.start()
    for out in outs:
        out.wait()


def per_device(th, tgain, head, sh, sgain, table, ec, ids):
    vmem, hbm = pl.BlockSpec(memory_space=pltpu.VMEM), pl.BlockSpec(memory_space=pl.ANY)
    found = pl.pallas_call(
        kernel,
        out_shape=(pltpu.VMEM(sh.shape, BF16), pltpu.VMEM(head.shape, BF16)),
        in_specs=[hbm] * 8,
        out_specs=(vmem, vmem),
        scratch_shapes=[
            *(pltpu.VMEM(small.shape, small.dtype) for small in (th, tgain, sh, sgain, ec, ids)),
            pltpu.VMEM((4, 2, 2, 4, 2, 48, 1024), BF16),
            pltpu.VMEM((4, 2, 2, 4, 2, 48, 512), BF16),
            pltpu.VMEM((4, 2, 2, 4, 2, 48, 512), BF16),
            pltpu.VMEM((4, 2, 2, 4, 48, 512), BF16),
            pltpu.VMEM(table.shape, BF16),
            pltpu.VMEM((3, 1024, 256), F32),
            pltpu.VMEM((3, 1024, 256), F32),
            pltpu.VMEM((3, 1024, 256), BF16),
            pltpu.VMEM((3, 256, 1024), BF16),
            pltpu.VMEM((3, 1024, 256), BF16),
            pltpu.VMEM((48, 512), F32),
            pltpu.VMEM((64, 512), BF16),
            pltpu.VMEM((64, 512), BF16),
            pltpu.VMEM((8, 8, 128), F32),
            pltpu.VMEM((48, 128), F32),
            pltpu.VMEM((3, 4, 8, 256), F32),
            pltpu.VMEM((3, 13, 8, 256), F32),
            pltpu.VMEM((4, 8, 256), F32),
            pltpu.VMEM((13, 8, 256), F32),
            *scatter_shapes(),
            pltpu.SemaphoreType.DMA((SENDS,)),
            pltpu.SemaphoreType.DMA((RECEIVES,)),
            pltpu.SemaphoreType.DMA((12,)),
            pltpu.SemaphoreType.DMA((12,)),
            pltpu.SemaphoreType.DMA((8,)),
        ],
        compiler_params=pltpu.CompilerParams(
            collective_id=0, has_side_effects=True, vmem_limit_bytes=54 * 1024 * 1024
        ),
        name="distill",
    )(th, tgain, head, sh, sgain, table, ec, ids)
    return pl.pallas_call(
        place_results,
        out_shape=(jax.ShapeDtypeStruct(sh.shape, BF16), jax.ShapeDtypeStruct(table.shape, BF16)),
        in_specs=[vmem, vmem],
        out_specs=(hbm, hbm),
        scratch_shapes=[pltpu.SemaphoreType.DMA((5,))],
        compiler_params=pltpu.CompilerParams(vmem_limit_bytes=32 * 1024 * 1024),
        name="place",
    )(*found)


def solution(mesh):
    return jax.shard_map(
        per_device,
        mesh=mesh,
        in_specs=(
            P("dp", "vocab"),
            P("vocab"),
            P(("dp", "vocab"), None),
            P("dp", "vocab"),
            P("vocab"),
            P(("dp", "vocab"), None),
            P("dp", "vocab"),
            P("dp"),
        ),
        out_specs=(P("dp", "vocab"), P(("dp", "vocab"), None)),
        check_vma=False,
    )
```

```python
import math

import jax
import jax.numpy as jnp
from jax import lax
from jax.experimental import pallas as pl
from jax.experimental.pallas import tpu as pltpu
from jax.sharding import PartitionSpec as P

MESH = pl.DeviceIdType.MESH
F32, BF16 = jnp.float32, jnp.bfloat16
ORDER = (("z", "x", "y"), ("x", "y", "z"), ("y", "z", "x"))
PARTS = (1, 2, 0)
SENDS, RECEIVES = 64, 174
NT = (((1,), (1,)), ((), ()))
NN = (((1,), (0,)), ((), ()))


def dot(a, b, dims=NN):
    return lax.dot_general(a, b, dims, preferred_element_type=F32)


class Place:
    def __init__(self):
        dp, vocab = lax.axis_index("dp"), lax.axis_index("vocab")
        self.vocab, self.dp = vocab, dp
        self.core = dp % 2
        self.at = {"x": (dp // 8) * 2 + vocab % 2, "y": (dp // 2) % 4, "z": vocab // 2}
        self.x_lo = vocab % 2

    def device(self, core=None, **moved):
        at = {**self.at, **moved}
        core = self.core if core is None else core
        return ((at["x"] // 2) * 8 + at["y"] * 2 + core, at["z"] * 2 + at["x"] % 2)

    def along(self, axis, by):
        return (self.at[axis] + by) % 4

    def shifted(self, axis, by):
        return self.device(**{axis: self.along(axis, by)})

    def sibling(self):
        return self.device(core=1 - self.core)


class Copies:
    def __init__(self, send_sems, recv_sems):
        self.send_sems, self.recv_sems, self.all = send_sems, recv_sems, []

    def start(self, src, dst, device):
        count = len(self.all)
        if count >= SENDS:
            self.all[count - SENDS].wait_send()
        copy = pltpu.make_async_remote_copy(
            src_ref=src,
            dst_ref=dst,
            send_sem=self.send_sems.at[count % SENDS],
            recv_sem=self.recv_sems.at[count],
            device_id=device,
            device_id_type=MESH,
        )
        copy.start()
        self.all.append(copy)
        return copy

    def finish(self):
        assert len(self.all) == RECEIVES, len(self.all)
        for copy in self.all[-SENDS:]:
            copy.wait_send()


def region(fixed, core, part, lanes):
    whole = slice(None)
    z, y = fixed.get("z", whole), fixed.get("y", whole)
    x_lo, x_hi = (fixed["x"] % 2, fixed["x"] // 2) if "x" in fixed else (whole, whole)
    return (z, x_lo, x_hi, y, core, pl.ds(16 * part, 16), lanes)


class Gather:
    def __init__(self, here, copies, buf, width):
        self.here, self.copies, self.buf, self.sibling = here, copies, buf, {}
        self.full, self.low, self.high = pl.ds(0, width), pl.ds(0, width // 2), pl.ds(width // 2, width // 2)

    def push(self, p, ph, by, lanes, device):
        here, axis = self.here, ORDER[p][ph]
        fixed = {a: here.at[a] for a in "xyz" if a not in ORDER[p][:ph]}
        fixed[axis] = here.along(axis, by)
        piece = self.buf.at[region(fixed, here.core, p, lanes)]
        return self.copies.start(piece, piece, device)

    def along(self, p, ph, by):
        return self.here.shifted(ORDER[p][ph], by)

    def to_sibling(self, p, by):
        self.sibling[p, by] = self.push(p, 2, by, self.full, self.here.sibling())

    def start_short(self, ph):
        self.short = [self.push(p, ph, 0, self.full, self.along(p, ph, by)) for by in (1, 3, 2) for p in PARTS]

    def wait_short(self):
        for copy in self.short:
            copy.wait_recv()

    def start_long(self, sibling=True):
        self.first = {
            (p, by): self.push(p, 2, 0, self.full, self.along(p, 2, by)) for p in PARTS for by in (1, -1)
        }
        if sibling:
            for p in PARTS:
                self.to_sibling(p, 0)

    def forward_long(self):
        self.second = []
        for p in PARTS:
            self.first[p, 1].wait_recv()
            self.second.append(self.push(p, 2, -1, self.low, self.along(p, 2, 1)))
            self.first[p, -1].wait_recv()
            self.second.append(self.push(p, 2, 1, self.high, self.along(p, 2, -1)))
        for p in PARTS:
            for by in (-1, 1):
                self.to_sibling(p, by)

    def finish_long(self):
        for p, right, left in zip(PARTS, self.second[::2], self.second[1::2]):
            right.wait_recv()
            left.wait_recv()
            self.to_sibling(p, 2)

    def wait_sibling(self, p, *moves):
        for by in moves or (0, -1, 1, 2):
            self.sibling[p, by].wait_recv()


def scatter(here, copies, p, buf, half, whole, direct, result):
    low, high, full = pl.ds(0, 256), pl.ds(256, 256), pl.ds(0, 512)
    order = ORDER[p][::-1]

    def slab(ph, by, lanes):
        fixed = {a: here.at[a] for a in order[:ph]}
        fixed[order[ph]] = here.along(order[ph], by)
        return region(fixed, here.core, p, lanes)

    right, left = here.shifted(order[0], 1), here.shifted(order[0], -1)
    first = (
        copies.start(buf.at[slab(0, 2, low)], half.at[0], right),
        copies.start(buf.at[slab(0, 2, high)], half.at[1], left),
    )
    yield
    first[0].wait_recv()
    at = slab(0, 1, low)
    buf[at] = (buf[at].astype(F32) + half[0].astype(F32)).astype(BF16)
    second = [copies.start(buf.at[slab(0, 1, full)], whole.at[0], right)]
    first[1].wait_recv()
    at = slab(0, -1, high)
    buf[at] = (buf[at].astype(F32) + half[1].astype(F32)).astype(BF16)
    second.append(copies.start(buf.at[slab(0, -1, full)], whole.at[1], left))
    yield
    for copy in second:
        copy.wait_recv()
    at = slab(0, 0, full)
    buf[at] = (buf[at].astype(F32) + whole[0].astype(F32) + whole[1].astype(F32)).astype(BF16)
    for ph, got in zip((1, 2), direct):
        sent = [
            copies.start(buf.at[slab(ph, by, full)], got.at[by - 1], here.shifted(order[ph], by)) for by in (1, 3, 2)
        ]
        yield
        total = buf[slab(ph, 0, full)].astype(F32)
        for copy in sent:
            copy.wait_recv()
        for i in range(3):
            total = total + got[i].astype(F32)
        if ph == 1:
            buf[slab(ph, 0, full)] = total.astype(BF16)
        else:
            result[pl.ds(16 * p, 16), :] = total


def scatter_shapes():
    sizes = {"x": (2, 2), "y": (4,), "z": (4,)}
    shapes = []
    for order in ORDER:
        left = ["x", "y", "z"]
        for ph, axis in enumerate(order[::-1]):
            left.remove(axis)
            dims = sum((sizes[a] for a in ("z", "x", "y") if a in left), ())
            if ph == 0:
                shapes.append(pltpu.VMEM((2, *dims, 16, 256), BF16))
            shapes.append(pltpu.VMEM((2 if ph == 0 else 3, *dims, 16, 512), BF16))
    return shapes


def totals(here, copies, sent, got):
    groups = (
        [here.device(core=core, x=here.along("x", by)) for core, by in OTHERS(here.core)],
        [here.shifted("y", by) for by in (1, 2, 3)],
        [here.shifted("z", by) for by in (1, 2, 3)],
    )
    slot = 0
    for step, targets in enumerate(groups):
        started = [copies.start(sent.at[step], got.at[slot + i], target) for i, target in enumerate(targets)]
        yield
        total = sent[step]
        for i, copy in enumerate(started):
            copy.wait_recv()
            total = total + got[slot + i]
        slot += len(targets)
        sent[step + 1] = total


def OTHERS(core):
    return [(1 - core, 0)] + [(c, by) for by in (1, 2, 3) for c in (core, 1 - core)]


def column_to_row(column):
    rows, lanes = lax.broadcasted_iota(jnp.int32, (48, 128), 0), lax.broadcasted_iota(jnp.int32, (48, 128), 1)
    return jnp.sum(jnp.where(rows == lanes, column, 0.0), axis=0, keepdims=True)


def row_to_column(row):
    rows, lanes = lax.broadcasted_iota(jnp.int32, (48, 128), 0), lax.broadcasted_iota(jnp.int32, (48, 128), 1)
    return jnp.sum(jnp.where(rows == lanes, row, 0.0), axis=1, keepdims=True)


def vocab_start(here, copies, slots, first_row, second_row):
    rows = lax.broadcasted_iota(jnp.int32, (8, 128), 0)
    slots[here.vocab] = jnp.where(rows == 0, first_row, jnp.where(rows == 1, second_row, 0.0))
    mine = slots.at[here.vocab]
    return [copies.start(mine, mine, (here.dp, (here.vocab + by) % 8)) for by in range(1, 8)]


def vocab_sum(slots, started):
    for copy in started:
        copy.wait_recv()
    total = slots[0]
    for slot in range(1, 8):
        total = total + slots[slot]
    return total


def kernel(
    th_hbm, tgain_hbm, head_hbm, sh_hbm, sgain_hbm, table_hbm, ec_hbm, ids_hbm,
    hidden_grad_ref, HEAD,
    TH, TGAIN, SH, SGAIN, EC, IDS,
    A, E, R, SB, ST, EXPT, SRAW, LGT, LG, OHT, GR, MSG, GOT, SQ, SCALE, TS, TR, TI, TIR,
    *rest,
):
    landing, (send_sems, recv_sems, sib_send, sib_recv, load_sems) = rest[:12], rest[12:]
    here = Place()
    copies = Copies(send_sems, recv_sems)
    x_lo = here.x_lo
    width = 3584

    barrier = pltpu.get_barrier_semaphore()
    partners = [here.shifted(axis, by) for axis in "yz" for by in (1, 2, 3)]
    partners += [here.device(core=core, x=here.along("x", by)) for core, by in OTHERS(here.core)]
    partners += [(here.dp, here.along("z", by) * 2 + 1 - x_lo) for by in (1, 2, 3)]
    for partner in partners:
        pl.semaphore_signal(barrier, inc=1, device_id=partner, device_id_type=MESH)

    loads = [
        pltpu.make_async_copy(src, dst, load_sems.at[i])
        for i, (src, dst) in enumerate(
            [(th_hbm, TH), (sh_hbm, SH), (tgain_hbm, TGAIN), (sgain_hbm, SGAIN), (ec_hbm, EC), (ids_hbm, IDS),
             (head_hbm, HEAD), (table_hbm, ST)]
        )
    ]
    for load in loads:
        load.start()
    for load in loads[:6]:
        load.wait()

    th, sh, ec = TH[...].astype(F32), SH[...].astype(F32), EC[...].astype(F32)
    tgain, sgain = TGAIN[...].reshape(1, 576).astype(F32), SGAIN[...].reshape(1, 448).astype(F32)
    low = x_lo == 0
    t_part = jnp.sum(th * th, axis=1, keepdims=True)
    s_part = jnp.sum(sh * sh, axis=1, keepdims=True)
    MSG[0:48, :] = jnp.concatenate([jnp.where(low, sh, th[:, :448]), ec[:, :64]], axis=1).astype(BF16)
    gain_row = jnp.concatenate([jnp.where(low, sgain, tgain[:, :448]), jnp.zeros((1, 64), F32)], axis=1)
    MSG[48:64, :] = jnp.broadcast_to(gain_row, (16, 512)).astype(BF16)
    t_row, s_row = column_to_row(t_part), column_to_row(s_part)
    pl.semaphore_wait(barrier, len(partners))
    started = vocab_start(here, copies, SQ, t_row, s_row)
    pair = copies.start(MSG, GOT, (here.dp, here.vocab + 1 - 2 * x_lo))
    sums = vocab_sum(SQ, started)
    t_scale = lax.rsqrt(row_to_column(sums[0:1]) / 4608 + 1e-06)
    s_scale = lax.rsqrt(row_to_column(sums[1:2]) / width + 1e-06)
    SCALE[...] = jnp.broadcast_to(s_scale, (48, 128))
    pair.wait_recv()
    got = GOT[0:48, :].astype(F32)
    got_gain = GOT[48:64, :].astype(F32)[0:1]

    values = jnp.where(
        low,
        jnp.concatenate([th, got[:, :448]], axis=1),
        jnp.concatenate([th[:, 448:], got[:, :448], sh], axis=1),
    )
    gains = jnp.where(
        low,
        jnp.concatenate([tgain, got_gain[:, :448]], axis=1),
        jnp.concatenate([tgain[:, 448:], got_gain[:, :448], sgain], axis=1),
    )
    lanes = lax.broadcasted_iota(jnp.int32, (48, 1024), 1)
    scales = jnp.where(jnp.logical_or(low, lanes < 128), t_scale, s_scale)
    own = (here.at["z"], x_lo, here.at["x"] // 2, here.at["y"], here.core)
    A[own] = (values * scales * gains).astype(BF16)

    states = Gather(here, copies, A, 1024)
    states.start_short(0)

    ids_row = IDS[...].reshape(1, 48).astype(F32)
    ids = row_to_column(jnp.concatenate([ids_row, jnp.zeros((1, 80), F32)], axis=1))
    spot = lax.broadcasted_iota(jnp.int32, (48, 128), 1)
    top = jnp.floor(ids * (1.0 / 4096.0))
    mid = jnp.floor((ids - 4096.0 * top) * (1.0 / 64.0))
    digits = jnp.where(
        spot == 0, top, jnp.where(spot == 1, mid, jnp.where(spot == 2, ids - 4096.0 * top - 64.0 * mid, 0.0))
    )
    E[own] = jnp.where(
        low,
        jnp.concatenate([ec, got[:, 448:]], axis=1),
        jnp.concatenate([ec[:, 64:], digits], axis=1),
    ).astype(BF16)

    cotangents = Gather(here, copies, E, 512)
    cotangents.start_short(0)
    states.wait_short()
    states.start_short(1)
    cotangents.wait_short()
    cotangents.start_short(1)
    states.wait_short()
    states.start_long()
    cotangents.wait_short()
    loads[6].wait()
    loads[7].wait()

    def part(ref, z, x, p, lo, hi):
        return ref[z, x, :, :, :, 16 * p : 16 * p + 16, lo:hi].reshape(256, hi - lo)

    def half_rows(m):
        return pl.ds(pl.multiple_of(m * 512, 512), 512)

    def squash(p, m, t_raw, s_raw):
        rows = half_rows(m)
        t_value = jnp.exp(30.0 * jnp.tanh(t_raw * (1.0 / 30.0)))
        s_value = jnp.exp(30.0 * jnp.tanh(s_raw * (1.0 / 30.0)))
        EXPT[p, rows, :] = t_value
        SRAW[p, rows, :] = s_raw
        sums = jnp.where(
            lax.broadcasted_iota(jnp.int32, (8, 256), 0) == 0,
            jnp.sum(t_value, axis=0, keepdims=True),
            jnp.sum(s_value, axis=0, keepdims=True),
        )
        TS[p, 0] = sums if m == 0 else TS[p, 0] + sums

    def block_logits(by, m, last=False):
        z = here.along("z", by)
        rows = half_rows(m)
        t_at, s_at = pl.multiple_of(z * 1152, 128), pl.multiple_of(z * 896, 128)
        t_raw = dot(HEAD[rows, pl.ds(t_at, 1024)], part(A, z, 0, 1, 0, 1024), NT)
        t_raw += dot(HEAD[rows, pl.ds(t_at + 1024, 128)], part(A, z, 1, 1, 0, 128), NT)
        s_raw = dot(ST[rows, pl.ds(s_at, 896)], part(A, z, 1, 1, 128, 1024), NT)
        if by != 0:
            t_raw += EXPT[1, rows, :]
            s_raw += SRAW[1, rows, :]
        if last:
            squash(1, m, t_raw, s_raw)
        else:
            EXPT[1, rows, :] = t_raw
            SRAW[1, rows, :] = s_raw

    def low_logits(p, m):
        rows = half_rows(m)
        return sum(dot(HEAD[rows, z * 1152 : z * 1152 + 1024], part(A, z, 0, p, 0, 1024), NT) for z in range(4))

    def high_logits(p, m):
        rows = half_rows(m)
        t_raw = dot(
            jnp.concatenate([HEAD[rows, z * 1152 + 1024 : z * 1152 + 1152] for z in range(4)], axis=1),
            jnp.concatenate([part(A, z, 1, p, 0, 128) for z in range(4)], axis=1),
            NT,
        )
        s_raw = dot(
            jnp.concatenate([ST[rows, z * 896 + 768 : z * 896 + 896] for z in range(4)], axis=1),
            jnp.concatenate([part(A, z, 1, p, 896, 1024) for z in range(4)], axis=1),
            NT,
        )
        for z in range(4):
            s_raw += dot(ST[rows, z * 896 : z * 896 + 768], part(A, z, 1, p, 128, 896), NT)
        return t_raw, s_raw

    def part_logits(p, m):
        t_raw, s_raw = high_logits(p, m)
        squash(p, m, t_raw + low_logits(p, m), s_raw)

    def early_logits(p, m):
        rows = half_rows(m)

        @pl.when(low)
        def _():
            EXPT[p, rows, :], SRAW[p, rows, :] = high_logits(p, m)

        @pl.when(jnp.logical_not(low))
        def _():
            EXPT[p, rows, :] = low_logits(p, m)

    def late_logits(p, m):
        rows = half_rows(m)

        @pl.when(low)
        def _():
            squash(p, m, EXPT[p, rows, :] + low_logits(p, m), SRAW[p, rows, :])

        @pl.when(jnp.logical_not(low))
        def _():
            t_raw, s_raw = high_logits(p, m)
            squash(p, m, EXPT[p, rows, :] + t_raw, s_raw)

    def start_totals(p):
        steps = totals(here, copies, TS.at[p], TR.at[p])
        next(steps)
        return steps

    def finish(steps):
        for _ in steps:
            pass

    states.wait_sibling(1, 0)
    for m in range(2):
        block_logits(0, m)
    states.forward_long()
    states.wait_sibling(1, -1, 1)
    for m in range(2):
        block_logits(-1, m)
        block_logits(1, m)
    states.wait_sibling(2, -1, 1)
    early_logits(2, 0)
    early_logits(2, 1)
    states.finish_long()
    cotangents.start_long(sibling=False)
    states.wait_sibling(1, 2)
    block_logits(2, 0, True)
    block_logits(2, 1, True)
    totals_of = {1: start_totals(1)}
    states.wait_sibling(2, 0, 2)
    late_logits(2, 0)
    late_logits(2, 1)
    for p in PARTS:
        cotangents.to_sibling(p, 0)
    cotangents.forward_long()
    next(totals_of[1])
    totals_of[2] = start_totals(2)
    states.wait_sibling(0)
    part_logits(0, 0)
    next(totals_of[1])
    next(totals_of[2])
    part_logits(0, 1)
    totals_of[0] = start_totals(0)
    finish(totals_of[1])
    cotangents.finish_long()

    def gradient(p):
        inverse = 1.0 / TS[p, 3]
        t_inverse, s_inverse = inverse[0:1], inverse[1:2]

        def step(m, total):
            rows = pl.ds(pl.multiple_of(m * 256, 256), 256)
            raw = SRAW[p, rows, :]
            tanh = jnp.tanh(raw * (1.0 / 30.0))
            grad = (jnp.exp(30.0 * tanh) * s_inverse - EXPT[p, rows, :] * t_inverse) * (1.0 - tanh * tanh)
            rounded = grad.astype(BF16)
            LGT[p, rows, :] = rounded
            LG[p, :, rows] = grad.T.astype(BF16)
            return total + jnp.sum(rounded.astype(F32) * raw, axis=0, keepdims=True)

        return lax.fori_loop(0, 4, step, jnp.zeros((1, 256), F32))

    def to_sibling(p, z):
        mine = pl.ds(16 * p, 16)
        return pltpu.make_async_remote_copy(
            src_ref=R.at[z, :, :, :, 1 - here.core, mine],
            dst_ref=SB.at[z, :, :, :, mine],
            send_sem=sib_send.at[p * 4 + z],
            recv_sem=sib_recv.at[p * 4 + z],
            device_id=here.sibling(),
            device_id_type=MESH,
        )

    def normed_grad(p, start, stop):
        def step(z, carry):
            for x in range(2):
                for half in range(2):
                    columns = pl.ds(pl.multiple_of(z * 896 + x * 384 + half * 256, 128), 256)
                    found = dot(LG[p], ST[:, columns]).astype(BF16)
                    R[z, x, :, :, :, 16 * p : 16 * p + 16, half * 256 : half * 256 + 256] = found.reshape(
                        2, 4, 2, 16, 256
                    )
            to_sibling(p, z).start()
            return carry

        lax.fori_loop(start, stop, step, 0)

    def start_scatter(p):
        def step(z, carry):
            to_sibling(p, z).wait_recv()
            at = (z, slice(None), slice(None), slice(None), here.core, pl.ds(16 * p, 16))
            mine = R[at].astype(F32) + SB[z, :, :, :, 16 * p : 16 * p + 16].astype(F32)
            R[at] = mine.astype(BF16)
            return carry

        lax.fori_loop(0, 4, step, 0)
        steps = scatter(
            here, copies, p, R, landing[4 * p], landing[4 * p + 1], landing[4 * p + 2 : 4 * p + 4], GR
        )
        next(steps)
        return steps

    inner_parts = {1: gradient(1)}
    normed_grad(1, 0, 2)
    next(totals_of[2])
    next(totals_of[0])
    normed_grad(1, 2, 4)
    finish(totals_of[2])
    scatters = {1: start_scatter(1)}
    inner_parts[2] = gradient(2)
    normed_grad(2, 0, 2)
    next(totals_of[0])
    normed_grad(2, 2, 4)
    scatters[2] = start_scatter(2)
    finish(totals_of[0])
    inner_parts[0] = gradient(0)

    which = lax.broadcasted_iota(jnp.int32, (8, 256), 0)
    TI[0] = jnp.where(which == 0, inner_parts[0], jnp.where(which == 1, inner_parts[1], inner_parts[2]))
    inner_steps = totals(here, copies, TI, TIR)
    next(inner_steps)
    normed_grad(0, 0, 2)
    next(scatters[1])
    next(inner_steps)
    normed_grad(0, 2, 4)
    scatters[0] = start_scatter(0)
    next(inner_steps)
    for p in PARTS:
        cotangents.wait_sibling(p)

    spot = lax.broadcasted_iota(jnp.int32, (8, 128), 1)
    weights = jnp.where(spot == 0, 4096.0, jnp.where(spot == 1, 64.0, jnp.where(spot == 2, 1.0, 0.0)))
    first_entry = ((here.dp * 8 + here.vocab) * 1024).astype(F32)

    def one_hot(p):
        token_row = dot(weights.astype(BF16), part(E, 0, 1, p, 384, 512), NT)[0:1] - first_entry

        def step(m, carry):
            rows = pl.ds(pl.multiple_of(m * 256, 256), 256)
            entry = (lax.broadcasted_iota(jnp.int32, (256, 256), 0) + m * 256).astype(F32)
            OHT[p, rows, :] = jnp.where(entry == token_row, 1.0, 0.0).astype(BF16)
            return carry

        lax.fori_loop(0, 4, step, 0)

    for p in PARTS:
        one_hot(p)

    def table_unit(z, x):
        size = 512 - 128 * x
        at = z * 896 + x * 512

        def step(m, carry):
            rows = half_rows(m)
            grads = jnp.concatenate([LGT[p, rows, :] for p in range(3)], axis=1)
            hot = jnp.concatenate([OHT[p, rows, :] for p in range(3)], axis=1)
            normed = jnp.concatenate(
                [part(A, z, 1, p, 128 + 512 * x, 128 + 512 * x + size) for p in range(3)], axis=0
            )
            cots = jnp.concatenate([part(E, z, x, p, 0, size) for p in range(3)], axis=0)
            found = dot(grads, normed) + math.sqrt(width) * dot(hot, cots)
            HEAD[rows, at : at + size] = found.astype(BF16)
            return carry

        lax.fori_loop(0, 2, step, 0)

    polls = {0: (2,), 1: (0,), 3: (1,), 4: (1, 2), 5: (0, 2), 6: (0,)}
    for unit in range(8):
        table_unit(unit // 2, unit % 2)
        for p in polls.get(unit, ()):
            next(scatters[p])
    finish(inner_steps)
    for p in (1, 2, 0):
        finish(scatters[p])

    found = GR[...]
    own_grad = jnp.where(low, found[:, :448], found[:, 64:])
    s_scale = SCALE[:, 0:1]
    lane = lax.broadcasted_iota(jnp.int32, (16, 256), 1) - lax.broadcasted_iota(jnp.int32, (16, 256), 0)
    inner = jnp.concatenate(
        [
            jnp.sum(jnp.where(lane == here.dp * 16, TI[3, p : p + 1, :], 0.0), axis=1, keepdims=True)
            for p in range(3)
        ],
        axis=0,
    )
    hidden_grad = s_scale * sgain * own_grad - sh * s_scale * s_scale * inner / width
    hidden_grad_ref[...] = hidden_grad.astype(BF16)

    copies.finish()
    for p in PARTS:
        for z in range(4):
            to_sibling(p, z).wait_send()


def place_results(hidden_from, table_from, hidden_to, table_to, out_sems):
    rows = table_from.shape[0] // 4
    columns = pl.ds(0, table_to.shape[1])
    pieces = [(table_from.at[at, columns], table_to.at[at]) for at in (pl.ds(i * rows, rows) for i in range(4))]
    pieces.append((hidden_from, hidden_to))
    outs = [pltpu.make_async_copy(a, b, out_sems.at[i]) for i, (a, b) in enumerate(pieces)]
    for out in outs:
        out.start()
    for out in outs:
        out.wait()


def per_device(th, tgain, head, sh, sgain, table, ec, ids):
    vmem, hbm = pl.BlockSpec(memory_space=pltpu.VMEM), pl.BlockSpec(memory_space=pl.ANY)
    found = pl.pallas_call(
        kernel,
        out_shape=(pltpu.VMEM(sh.shape, BF16), pltpu.VMEM(head.shape, BF16)),
        in_specs=[hbm] * 8,
        out_specs=(vmem, vmem),
        scratch_shapes=[
            *(pltpu.VMEM(small.shape, small.dtype) for small in (th, tgain, sh, sgain, ec, ids)),
            pltpu.VMEM((4, 2, 2, 4, 2, 48, 1024), BF16),
            pltpu.VMEM((4, 2, 2, 4, 2, 48, 512), BF16),
            pltpu.VMEM((4, 2, 2, 4, 2, 48, 512), BF16),
            pltpu.VMEM((4, 2, 2, 4, 48, 512), BF16),
            pltpu.VMEM(table.shape, BF16),
            pltpu.VMEM((3, 1024, 256), F32),
            pltpu.VMEM((3, 1024, 256), F32),
            pltpu.VMEM((3, 1024, 256), BF16),
            pltpu.VMEM((3, 256, 1024), BF16),
            pltpu.VMEM((3, 1024, 256), BF16),
            pltpu.VMEM((48, 512), F32),
            pltpu.VMEM((64, 512), BF16),
            pltpu.VMEM((64, 512), BF16),
            pltpu.VMEM((8, 8, 128), F32),
            pltpu.VMEM((48, 128), F32),
            pltpu.VMEM((3, 4, 8, 256), F32),
            pltpu.VMEM((3, 13, 8, 256), F32),
            pltpu.VMEM((4, 8, 256), F32),
            pltpu.VMEM((13, 8, 256), F32),
            *scatter_shapes(),
            pltpu.SemaphoreType.DMA((SENDS,)),
            pltpu.SemaphoreType.DMA((RECEIVES,)),
            pltpu.SemaphoreType.DMA((12,)),
            pltpu.SemaphoreType.DMA((12,)),
            pltpu.SemaphoreType.DMA((8,)),
        ],
        compiler_params=pltpu.CompilerParams(
            collective_id=0, has_side_effects=True, vmem_limit_bytes=54 * 1024 * 1024
        ),
        name="distill",
    )(th, tgain, head, sh, sgain, table, ec, ids)
    return pl.pallas_call(
        place_results,
        out_shape=(jax.ShapeDtypeStruct(sh.shape, BF16), jax.ShapeDtypeStruct(table.shape, BF16)),
        in_specs=[vmem, vmem],
        out_specs=(hbm, hbm),
        scratch_shapes=[pltpu.SemaphoreType.DMA((5,))],
        compiler_params=pltpu.CompilerParams(vmem_limit_bytes=32 * 1024 * 1024),
        name="place",
    )(*found)


def solution(mesh):
    return jax.shard_map(
        per_device,
        mesh=mesh,
        in_specs=(
            P("dp", "vocab"),
            P("vocab"),
            P(("dp", "vocab"), None),
            P("dp", "vocab"),
            P("vocab"),
            P(("dp", "vocab"), None),
            P("dp", "vocab"),
            P("dp"),
        ),
        out_specs=(P("dp", "vocab"), P(("dp", "vocab"), None)),
        check_vma=False,
    )
```

```python
import math

import jax
import jax.numpy as jnp
from jax import lax
from jax.experimental import pallas as pl
from jax.experimental.pallas import tpu as pltpu
from jax.sharding import PartitionSpec as P

MESH = pl.DeviceIdType.MESH
F32, BF16 = jnp.float32, jnp.bfloat16
ORDER = (("z", "x", "y"), ("x", "y", "z"), ("y", "z", "x"))
PARTS = (1, 2, 0)
SENDS, RECEIVES = 64, 174
NT = (((1,), (1,)), ((), ()))
NN = (((1,), (0,)), ((), ()))


def dot(a, b, dims=NN):
    return lax.dot_general(a, b, dims, preferred_element_type=F32)


class Place:
    def __init__(self):
        dp, vocab = lax.axis_index("dp"), lax.axis_index("vocab")
        self.vocab, self.dp = vocab, dp
        self.core = dp % 2
        self.at = {"x": (dp // 8) * 2 + vocab % 2, "y": (dp // 2) % 4, "z": vocab // 2}
        self.x_lo = vocab % 2

    def device(self, core=None, **moved):
        at = {**self.at, **moved}
        core = self.core if core is None else core
        return ((at["x"] // 2) * 8 + at["y"] * 2 + core, at["z"] * 2 + at["x"] % 2)

    def along(self, axis, by):
        return (self.at[axis] + by) % 4

    def shifted(self, axis, by):
        return self.device(**{axis: self.along(axis, by)})

    def sibling(self):
        return self.device(core=1 - self.core)


class Copies:
    def __init__(self, send_sems, recv_sems):
        self.send_sems, self.recv_sems, self.all = send_sems, recv_sems, []

    def start(self, src, dst, device):
        count = len(self.all)
        if count >= SENDS:
            self.all[count - SENDS].wait_send()
        copy = pltpu.make_async_remote_copy(
            src_ref=src,
            dst_ref=dst,
            send_sem=self.send_sems.at[count % SENDS],
            recv_sem=self.recv_sems.at[count],
            device_id=device,
            device_id_type=MESH,
        )
        copy.start()
        self.all.append(copy)
        return copy

    def finish(self):
        assert len(self.all) == RECEIVES, len(self.all)
        for copy in self.all[-SENDS:]:
            copy.wait_send()


def region(fixed, core, part, lanes):
    whole = slice(None)
    z, y = fixed.get("z", whole), fixed.get("y", whole)
    x_lo, x_hi = (fixed["x"] % 2, fixed["x"] // 2) if "x" in fixed else (whole, whole)
    return (z, x_lo, x_hi, y, core, pl.ds(16 * part, 16), lanes)


class Gather:
    def __init__(self, here, copies, buf, width):
        self.here, self.copies, self.buf, self.sibling = here, copies, buf, {}
        self.full, self.low, self.high = pl.ds(0, width), pl.ds(0, width // 2), pl.ds(width // 2, width // 2)

    def push(self, p, ph, by, lanes, device):
        here, axis = self.here, ORDER[p][ph]
        fixed = {a: here.at[a] for a in "xyz" if a not in ORDER[p][:ph]}
        fixed[axis] = here.along(axis, by)
        piece = self.buf.at[region(fixed, here.core, p, lanes)]
        return self.copies.start(piece, piece, device)

    def along(self, p, ph, by):
        return self.here.shifted(ORDER[p][ph], by)

    def to_sibling(self, p, by):
        self.sibling[p, by] = self.push(p, 2, by, self.full, self.here.sibling())

    def start_short(self, ph):
        self.short = [self.push(p, ph, 0, self.full, self.along(p, ph, by)) for by in (1, 3, 2) for p in PARTS]

    def wait_short(self):
        for copy in self.short:
            copy.wait_recv()

    def start_long(self, sibling=True):
        self.first = {
            (p, by): self.push(p, 2, 0, self.full, self.along(p, 2, by)) for p in PARTS for by in (1, -1)
        }
        if sibling:
            for p in PARTS:
                self.to_sibling(p, 0)

    def forward_long(self):
        self.second = []
        for p in PARTS:
            self.first[p, 1].wait_recv()
            self.second.append(self.push(p, 2, -1, self.low, self.along(p, 2, 1)))
            self.first[p, -1].wait_recv()
            self.second.append(self.push(p, 2, 1, self.high, self.along(p, 2, -1)))
        for p in PARTS:
            for by in (-1, 1):
                self.to_sibling(p, by)

    def finish_long(self):
        for p, right, left in zip(PARTS, self.second[::2], self.second[1::2]):
            right.wait_recv()
            left.wait_recv()
            self.to_sibling(p, 2)

    def wait_sibling(self, p, *moves):
        for by in moves or (0, -1, 1, 2):
            self.sibling[p, by].wait_recv()


def scatter(here, copies, p, buf, half, whole, direct, result):
    low, high, full = pl.ds(0, 256), pl.ds(256, 256), pl.ds(0, 512)
    order = ORDER[p][::-1]

    def slab(ph, by, lanes):
        fixed = {a: here.at[a] for a in order[:ph]}
        fixed[order[ph]] = here.along(order[ph], by)
        return region(fixed, here.core, p, lanes)

    right, left = here.shifted(order[0], 1), here.shifted(order[0], -1)
    first = (
        copies.start(buf.at[slab(0, 2, low)], half.at[0], right),
        copies.start(buf.at[slab(0, 2, high)], half.at[1], left),
    )
    yield
    first[0].wait_recv()
    at = slab(0, 1, low)
    buf[at] = (buf[at].astype(F32) + half[0].astype(F32)).astype(BF16)
    second = [copies.start(buf.at[slab(0, 1, full)], whole.at[0], right)]
    first[1].wait_recv()
    at = slab(0, -1, high)
    buf[at] = (buf[at].astype(F32) + half[1].astype(F32)).astype(BF16)
    second.append(copies.start(buf.at[slab(0, -1, full)], whole.at[1], left))
    yield
    for copy in second:
        copy.wait_recv()
    at = slab(0, 0, full)
    buf[at] = (buf[at].astype(F32) + whole[0].astype(F32) + whole[1].astype(F32)).astype(BF16)
    for ph, got in zip((1, 2), direct):
        sent = [
            copies.start(buf.at[slab(ph, by, full)], got.at[by - 1], here.shifted(order[ph], by)) for by in (1, 3, 2)
        ]
        yield
        total = buf[slab(ph, 0, full)].astype(F32)
        for copy in sent:
            copy.wait_recv()
        for i in range(3):
            total = total + got[i].astype(F32)
        if ph == 1:
            buf[slab(ph, 0, full)] = total.astype(BF16)
        else:
            result[pl.ds(16 * p, 16), :] = total


def scatter_shapes():
    sizes = {"x": (2, 2), "y": (4,), "z": (4,)}
    shapes = []
    for order in ORDER:
        left = ["x", "y", "z"]
        for ph, axis in enumerate(order[::-1]):
            left.remove(axis)
            dims = sum((sizes[a] for a in ("z", "x", "y") if a in left), ())
            if ph == 0:
                shapes.append(pltpu.VMEM((2, *dims, 16, 256), BF16))
            shapes.append(pltpu.VMEM((2 if ph == 0 else 3, *dims, 16, 512), BF16))
    return shapes


def totals(here, copies, sent, got):
    groups = (
        [here.device(core=core, x=here.along("x", by)) for core, by in OTHERS(here.core)],
        [here.shifted("y", by) for by in (1, 2, 3)],
        [here.shifted("z", by) for by in (1, 2, 3)],
    )
    slot = 0
    for step, targets in enumerate(groups):
        started = [copies.start(sent.at[step], got.at[slot + i], target) for i, target in enumerate(targets)]
        yield
        total = sent[step]
        for i, copy in enumerate(started):
            copy.wait_recv()
            total = total + got[slot + i]
        slot += len(targets)
        sent[step + 1] = total


def OTHERS(core):
    return [(1 - core, 0)] + [(c, by) for by in (1, 2, 3) for c in (core, 1 - core)]


def column_to_row(column):
    rows, lanes = lax.broadcasted_iota(jnp.int32, (48, 128), 0), lax.broadcasted_iota(jnp.int32, (48, 128), 1)
    return jnp.sum(jnp.where(rows == lanes, column, 0.0), axis=0, keepdims=True)


def row_to_column(row):
    rows, lanes = lax.broadcasted_iota(jnp.int32, (48, 128), 0), lax.broadcasted_iota(jnp.int32, (48, 128), 1)
    return jnp.sum(jnp.where(rows == lanes, row, 0.0), axis=1, keepdims=True)


def vocab_start(here, copies, slots, first_row, second_row):
    rows = lax.broadcasted_iota(jnp.int32, (8, 128), 0)
    slots[here.vocab] = jnp.where(rows == 0, first_row, jnp.where(rows == 1, second_row, 0.0))
    mine = slots.at[here.vocab]
    return [copies.start(mine, mine, (here.dp, (here.vocab + by) % 8)) for by in range(1, 8)]


def vocab_sum(slots, started):
    for copy in started:
        copy.wait_recv()
    total = slots[0]
    for slot in range(1, 8):
        total = total + slots[slot]
    return total


def kernel(
    th_hbm, tgain_hbm, head_hbm, sh_hbm, sgain_hbm, table_hbm, ec_hbm, ids_hbm,
    hidden_grad_ref, HEAD,
    TH, TGAIN, SH, SGAIN, EC, IDS,
    A, E, R, SB, ST, EXPT, SRAW, LGT, LG, OHT, GR, MSG, GOT, SQ, SCALE, TS, TR, TI, TIR,
    *rest,
):
    landing, (send_sems, recv_sems, sib_send, sib_recv, load_sems) = rest[:12], rest[12:]
    here = Place()
    copies = Copies(send_sems, recv_sems)
    x_lo = here.x_lo
    width = 3584

    barrier = pltpu.get_barrier_semaphore()
    partners = [here.shifted(axis, by) for axis in "yz" for by in (1, 2, 3)]
    partners += [here.device(core=core, x=here.along("x", by)) for core, by in OTHERS(here.core)]
    partners += [(here.dp, here.along("z", by) * 2 + 1 - x_lo) for by in (1, 2, 3)]
    for partner in partners:
        pl.semaphore_signal(barrier, inc=1, device_id=partner, device_id_type=MESH)

    loads = [
        pltpu.make_async_copy(src, dst, load_sems.at[i])
        for i, (src, dst) in enumerate(
            [(th_hbm, TH), (sh_hbm, SH), (tgain_hbm, TGAIN), (sgain_hbm, SGAIN), (ec_hbm, EC), (ids_hbm, IDS),
             (head_hbm, HEAD), (table_hbm, ST)]
        )
    ]
    for load in loads:
        load.start()
    for load in loads[:6]:
        load.wait()

    th, sh, ec = TH[...].astype(F32), SH[...].astype(F32), EC[...].astype(F32)
    tgain, sgain = TGAIN[...].reshape(1, 576).astype(F32), SGAIN[...].reshape(1, 448).astype(F32)
    low = x_lo == 0
    t_part = jnp.sum(th * th, axis=1, keepdims=True)
    s_part = jnp.sum(sh * sh, axis=1, keepdims=True)
    MSG[0:48, :] = jnp.concatenate([jnp.where(low, sh, th[:, :448]), ec[:, :64]], axis=1).astype(BF16)
    gain_row = jnp.concatenate([jnp.where(low, sgain, tgain[:, :448]), jnp.zeros((1, 64), F32)], axis=1)
    MSG[48:64, :] = jnp.broadcast_to(gain_row, (16, 512)).astype(BF16)
    t_row, s_row = column_to_row(t_part), column_to_row(s_part)
    pl.semaphore_wait(barrier, len(partners))
    started = vocab_start(here, copies, SQ, t_row, s_row)
    pair = copies.start(MSG, GOT, (here.dp, here.vocab + 1 - 2 * x_lo))
    sums = vocab_sum(SQ, started)
    t_scale = lax.rsqrt(row_to_column(sums[0:1]) / 4608 + 1e-06)
    s_scale = lax.rsqrt(row_to_column(sums[1:2]) / width + 1e-06)
    SCALE[...] = jnp.broadcast_to(s_scale, (48, 128))
    pair.wait_recv()
    got = GOT[0:48, :].astype(F32)
    got_gain = GOT[48:64, :].astype(F32)[0:1]

    values = jnp.where(
        low,
        jnp.concatenate([th, got[:, :448]], axis=1),
        jnp.concatenate([th[:, 448:], got[:, :448], sh], axis=1),
    )
    gains = jnp.where(
        low,
        jnp.concatenate([tgain, got_gain[:, :448]], axis=1),
        jnp.concatenate([tgain[:, 448:], got_gain[:, :448], sgain], axis=1),
    )
    lanes = lax.broadcasted_iota(jnp.int32, (48, 1024), 1)
    scales = jnp.where(jnp.logical_or(low, lanes < 128), t_scale, s_scale)
    own = (here.at["z"], x_lo, here.at["x"] // 2, here.at["y"], here.core)
    A[own] = (values * scales * gains).astype(BF16)

    states = Gather(here, copies, A, 1024)
    states.start_short(0)

    ids_row = IDS[...].reshape(1, 48).astype(F32)
    ids = row_to_column(jnp.concatenate([ids_row, jnp.zeros((1, 80), F32)], axis=1))
    spot = lax.broadcasted_iota(jnp.int32, (48, 128), 1)
    top = jnp.floor(ids * (1.0 / 4096.0))
    mid = jnp.floor((ids - 4096.0 * top) * (1.0 / 64.0))
    digits = jnp.where(
        spot == 0, top, jnp.where(spot == 1, mid, jnp.where(spot == 2, ids - 4096.0 * top - 64.0 * mid, 0.0))
    )
    E[own] = jnp.where(
        low,
        jnp.concatenate([ec, got[:, 448:]], axis=1),
        jnp.concatenate([ec[:, 64:], digits], axis=1),
    ).astype(BF16)

    cotangents = Gather(here, copies, E, 512)
    cotangents.start_short(0)
    states.wait_short()
    states.start_short(1)
    cotangents.wait_short()
    cotangents.start_short(1)
    states.wait_short()
    states.start_long()
    cotangents.wait_short()
    loads[6].wait()
    loads[7].wait()

    def part(ref, z, x, p, lo, hi):
        return ref[z, x, :, :, :, 16 * p : 16 * p + 16, lo:hi].reshape(256, hi - lo)

    def half_rows(m):
        return pl.ds(pl.multiple_of(m * 512, 512), 512)

    def squash(p, m, t_raw, s_raw):
        rows = half_rows(m)
        t_value = jnp.exp(30.0 * jnp.tanh(t_raw * (1.0 / 30.0)))
        s_value = jnp.exp(30.0 * jnp.tanh(s_raw * (1.0 / 30.0)))
        EXPT[p, rows, :] = t_value
        SRAW[p, rows, :] = s_raw
        sums = jnp.where(
            lax.broadcasted_iota(jnp.int32, (8, 256), 0) == 0,
            jnp.sum(t_value, axis=0, keepdims=True),
            jnp.sum(s_value, axis=0, keepdims=True),
        )
        TS[p, 0] = sums if m == 0 else TS[p, 0] + sums

    def block_logits(by, m, last=False):
        z = here.along("z", by)
        rows = half_rows(m)
        t_at, s_at = pl.multiple_of(z * 1152, 128), pl.multiple_of(z * 896, 128)
        t_raw = dot(HEAD[rows, pl.ds(t_at, 1024)], part(A, z, 0, 1, 0, 1024), NT)
        t_raw += dot(HEAD[rows, pl.ds(t_at + 1024, 128)], part(A, z, 1, 1, 0, 128), NT)
        s_raw = dot(ST[rows, pl.ds(s_at, 896)], part(A, z, 1, 1, 128, 1024), NT)
        if by != 0:
            t_raw += EXPT[1, rows, :]
            s_raw += SRAW[1, rows, :]
        if last:
            squash(1, m, t_raw, s_raw)
        else:
            EXPT[1, rows, :] = t_raw
            SRAW[1, rows, :] = s_raw

    def low_logits(p, m):
        rows = half_rows(m)
        return sum(dot(HEAD[rows, z * 1152 : z * 1152 + 1024], part(A, z, 0, p, 0, 1024), NT) for z in range(4))

    def high_logits(p, m):
        rows = half_rows(m)
        t_raw = dot(
            jnp.concatenate([HEAD[rows, z * 1152 + 1024 : z * 1152 + 1152] for z in range(4)], axis=1),
            jnp.concatenate([part(A, z, 1, p, 0, 128) for z in range(4)], axis=1),
            NT,
        )
        s_raw = dot(
            jnp.concatenate([ST[rows, z * 896 + 768 : z * 896 + 896] for z in range(4)], axis=1),
            jnp.concatenate([part(A, z, 1, p, 896, 1024) for z in range(4)], axis=1),
            NT,
        )
        for z in range(4):
            s_raw += dot(ST[rows, z * 896 : z * 896 + 768], part(A, z, 1, p, 128, 896), NT)
        return t_raw, s_raw

    def part_logits(p, m):
        t_raw, s_raw = high_logits(p, m)
        squash(p, m, t_raw + low_logits(p, m), s_raw)

    def early_logits(p, m):
        rows = half_rows(m)

        @pl.when(low)
        def _():
            EXPT[p, rows, :], SRAW[p, rows, :] = high_logits(p, m)

        @pl.when(jnp.logical_not(low))
        def _():
            EXPT[p, rows, :] = low_logits(p, m)

    def late_logits(p, m):
        rows = half_rows(m)

        @pl.when(low)
        def _():
            squash(p, m, EXPT[p, rows, :] + low_logits(p, m), SRAW[p, rows, :])

        @pl.when(jnp.logical_not(low))
        def _():
            t_raw, s_raw = high_logits(p, m)
            squash(p, m, EXPT[p, rows, :] + t_raw, s_raw)

    def start_totals(p):
        steps = totals(here, copies, TS.at[p], TR.at[p])
        next(steps)
        return steps

    def finish(steps):
        for _ in steps:
            pass

    states.wait_sibling(1, 0)
    for m in range(2):
        block_logits(0, m)
    states.forward_long()
    states.wait_sibling(1, -1, 1)
    for m in range(2):
        block_logits(-1, m)
        block_logits(1, m)
    states.wait_sibling(2, -1, 1)
    early_logits(2, 0)
    early_logits(2, 1)
    states.finish_long()
    cotangents.start_long(sibling=False)
    states.wait_sibling(1, 2)
    block_logits(2, 0, True)
    block_logits(2, 1, True)
    totals_of = {1: start_totals(1)}
    states.wait_sibling(2, 0, 2)
    late_logits(2, 0)
    late_logits(2, 1)
    for p in PARTS:
        cotangents.to_sibling(p, 0)
    cotangents.forward_long()
    next(totals_of[1])
    totals_of[2] = start_totals(2)
    states.wait_sibling(0)
    part_logits(0, 0)
    next(totals_of[1])
    next(totals_of[2])
    part_logits(0, 1)
    totals_of[0] = start_totals(0)
    finish(totals_of[1])
    cotangents.finish_long()

    def gradient(p):
        inverse = 1.0 / TS[p, 3]
        t_inverse, s_inverse = inverse[0:1], inverse[1:2]

        def step(m, total):
            rows = pl.ds(pl.multiple_of(m * 256, 256), 256)
            raw = SRAW[p, rows, :]
            tanh = jnp.tanh(raw * (1.0 / 30.0))
            grad = (jnp.exp(30.0 * tanh) * s_inverse - EXPT[p, rows, :] * t_inverse) * (1.0 - tanh * tanh)
            rounded = grad.astype(BF16)
            LGT[p, rows, :] = rounded
            LG[p, :, rows] = grad.T.astype(BF16)
            return total + jnp.sum(rounded.astype(F32) * raw, axis=0, keepdims=True)

        return lax.fori_loop(0, 4, step, jnp.zeros((1, 256), F32))

    def to_sibling(p, z):
        mine = pl.ds(16 * p, 16)
        return pltpu.make_async_remote_copy(
            src_ref=R.at[z, :, :, :, 1 - here.core, mine],
            dst_ref=SB.at[z, :, :, :, mine],
            send_sem=sib_send.at[p * 4 + z],
            recv_sem=sib_recv.at[p * 4 + z],
            device_id=here.sibling(),
            device_id_type=MESH,
        )

    def normed_grad(p, start, stop):
        def step(z, carry):
            for x in range(2):
                for half in range(2):
                    columns = pl.ds(pl.multiple_of(z * 896 + x * 384 + half * 256, 128), 256)
                    found = dot(LG[p], ST[:, columns]).astype(BF16)
                    R[z, x, :, :, :, 16 * p : 16 * p + 16, half * 256 : half * 256 + 256] = found.reshape(
                        2, 4, 2, 16, 256
                    )
            to_sibling(p, z).start()
            return carry

        lax.fori_loop(start, stop, step, 0)

    def start_scatter(p):
        def step(z, carry):
            to_sibling(p, z).wait_recv()
            at = (z, slice(None), slice(None), slice(None), here.core, pl.ds(16 * p, 16))
            mine = R[at].astype(F32) + SB[z, :, :, :, 16 * p : 16 * p + 16].astype(F32)
            R[at] = mine.astype(BF16)
            return carry

        lax.fori_loop(0, 4, step, 0)
        steps = scatter(
            here, copies, p, R, landing[4 * p], landing[4 * p + 1], landing[4 * p + 2 : 4 * p + 4], GR
        )
        next(steps)
        return steps

    inner_parts = {1: gradient(1)}
    next(totals_of[2])
    normed_grad(1, 0, 4)
    next(totals_of[0])
    scatters = {1: start_scatter(1)}
    finish(totals_of[2])
    inner_parts[2] = gradient(2)
    normed_grad(2, 0, 2)
    next(totals_of[0])
    normed_grad(2, 2, 4)
    scatters[2] = start_scatter(2)
    finish(totals_of[0])
    inner_parts[0] = gradient(0)

    which = lax.broadcasted_iota(jnp.int32, (8, 256), 0)
    TI[0] = jnp.where(which == 0, inner_parts[0], jnp.where(which == 1, inner_parts[1], inner_parts[2]))
    inner_steps = totals(here, copies, TI, TIR)
    next(inner_steps)
    normed_grad(0, 0, 4)
    scatters[0] = start_scatter(0)
    next(scatters[1])
    next(inner_steps)
    scatters["inner"] = inner_steps
    for p in PARTS:
        cotangents.wait_sibling(p)

    spot = lax.broadcasted_iota(jnp.int32, (8, 128), 1)
    weights = jnp.where(spot == 0, 4096.0, jnp.where(spot == 1, 64.0, jnp.where(spot == 2, 1.0, 0.0)))
    first_entry = ((here.dp * 8 + here.vocab) * 1024).astype(F32)

    def one_hot(p):
        token_row = dot(weights.astype(BF16), part(E, 0, 1, p, 384, 512), NT)[0:1] - first_entry

        def step(m, carry):
            rows = pl.ds(pl.multiple_of(m * 256, 256), 256)
            entry = (lax.broadcasted_iota(jnp.int32, (256, 256), 0) + m * 256).astype(F32)
            OHT[p, rows, :] = jnp.where(entry == token_row, 1.0, 0.0).astype(BF16)
            return carry

        lax.fori_loop(0, 4, step, 0)

    for p in PARTS:
        one_hot(p)

    def table_unit(z, x):
        size = 512 - 128 * x
        at = z * 896 + x * 512

        def step(m, carry):
            rows = half_rows(m)
            grads = jnp.concatenate([LGT[p, rows, :] for p in range(3)], axis=1)
            hot = jnp.concatenate([OHT[p, rows, :] for p in range(3)], axis=1)
            normed = jnp.concatenate(
                [part(A, z, 1, p, 128 + 512 * x, 128 + 512 * x + size) for p in range(3)], axis=0
            )
            cots = jnp.concatenate([part(E, z, x, p, 0, size) for p in range(3)], axis=0)
            found = dot(grads, normed) + math.sqrt(width) * dot(hot, cots)
            HEAD[rows, at : at + size] = found.astype(BF16)
            return carry

        lax.fori_loop(0, 2, step, 0)

    polls = {0: (2,), 1: (0, "inner"), 3: (1,), 4: (1, 2), 5: (0, 2), 6: (0,)}
    for unit in range(8):
        table_unit(unit // 2, unit % 2)
        for p in polls.get(unit, ()):
            next(scatters[p])
    finish(inner_steps)
    for p in (1, 2, 0):
        finish(scatters[p])

    found = GR[...]
    own_grad = jnp.where(low, found[:, :448], found[:, 64:])
    s_scale = SCALE[:, 0:1]
    lane = lax.broadcasted_iota(jnp.int32, (16, 256), 1) - lax.broadcasted_iota(jnp.int32, (16, 256), 0)
    inner = jnp.concatenate(
        [
            jnp.sum(jnp.where(lane == here.dp * 16, TI[3, p : p + 1, :], 0.0), axis=1, keepdims=True)
            for p in range(3)
        ],
        axis=0,
    )
    hidden_grad = s_scale * sgain * own_grad - sh * s_scale * s_scale * inner / width
    hidden_grad_ref[...] = hidden_grad.astype(BF16)

    copies.finish()
    for p in PARTS:
        for z in range(4):
            to_sibling(p, z).wait_send()


def place_results(hidden_from, table_from, hidden_to, table_to, out_sems):
    rows = table_from.shape[0] // 4
    columns = pl.ds(0, table_to.shape[1])
    pieces = [(table_from.at[at, columns], table_to.at[at]) for at in (pl.ds(i * rows, rows) for i in range(4))]
    pieces.append((hidden_from, hidden_to))
    outs = [pltpu.make_async_copy(a, b, out_sems.at[i]) for i, (a, b) in enumerate(pieces)]
    for out in outs:
        out.start()
    for out in outs:
        out.wait()


def per_device(th, tgain, head, sh, sgain, table, ec, ids):
    vmem, hbm = pl.BlockSpec(memory_space=pltpu.VMEM), pl.BlockSpec(memory_space=pl.ANY)
    found = pl.pallas_call(
        kernel,
        out_shape=(pltpu.VMEM(sh.shape, BF16), pltpu.VMEM(head.shape, BF16)),
        in_specs=[hbm] * 8,
        out_specs=(vmem, vmem),
        scratch_shapes=[
            *(pltpu.VMEM(small.shape, small.dtype) for small in (th, tgain, sh, sgain, ec, ids)),
            pltpu.VMEM((4, 2, 2, 4, 2, 48, 1024), BF16),
            pltpu.VMEM((4, 2, 2, 4, 2, 48, 512), BF16),
            pltpu.VMEM((4, 2, 2, 4, 2, 48, 512), BF16),
            pltpu.VMEM((4, 2, 2, 4, 48, 512), BF16),
            pltpu.VMEM(table.shape, BF16),
            pltpu.VMEM((3, 1024, 256), F32),
            pltpu.VMEM((3, 1024, 256), F32),
            pltpu.VMEM((3, 1024, 256), BF16),
            pltpu.VMEM((3, 256, 1024), BF16),
            pltpu.VMEM((3, 1024, 256), BF16),
            pltpu.VMEM((48, 512), F32),
            pltpu.VMEM((64, 512), BF16),
            pltpu.VMEM((64, 512), BF16),
            pltpu.VMEM((8, 8, 128), F32),
            pltpu.VMEM((48, 128), F32),
            pltpu.VMEM((3, 4, 8, 256), F32),
            pltpu.VMEM((3, 13, 8, 256), F32),
            pltpu.VMEM((4, 8, 256), F32),
            pltpu.VMEM((13, 8, 256), F32),
            *scatter_shapes(),
            pltpu.SemaphoreType.DMA((SENDS,)),
            pltpu.SemaphoreType.DMA((RECEIVES,)),
            pltpu.SemaphoreType.DMA((12,)),
            pltpu.SemaphoreType.DMA((12,)),
            pltpu.SemaphoreType.DMA((8,)),
        ],
        compiler_params=pltpu.CompilerParams(
            collective_id=0, has_side_effects=True, vmem_limit_bytes=54 * 1024 * 1024
        ),
        name="distill",
    )(th, tgain, head, sh, sgain, table, ec, ids)
    return pl.pallas_call(
        place_results,
        out_shape=(jax.ShapeDtypeStruct(sh.shape, BF16), jax.ShapeDtypeStruct(table.shape, BF16)),
        in_specs=[vmem, vmem],
        out_specs=(hbm, hbm),
        scratch_shapes=[pltpu.SemaphoreType.DMA((5,))],
        compiler_params=pltpu.CompilerParams(vmem_limit_bytes=32 * 1024 * 1024),
        name="place",
    )(*found)


def solution(mesh):
    return jax.shard_map(
        per_device,
        mesh=mesh,
        in_specs=(
            P("dp", "vocab"),
            P("vocab"),
            P(("dp", "vocab"), None),
            P("dp", "vocab"),
            P("vocab"),
            P(("dp", "vocab"), None),
            P("dp", "vocab"),
            P("dp"),
        ),
        out_specs=(P("dp", "vocab"), P(("dp", "vocab"), None)),
        check_vma=False,
    )
```
